32 devices in a mesh: seq: 8 (over z, x), head: 4 (over y, core).
Axes of the slice: x: 2, y: 2, z: 4, core: 2. Of those that a mesh axis runs over, the one named last changes fastest.
Arguments:
- queries: bfloat16 [768, 8192], P('head', 'seq'), may hold values from -6 to 6
- keys: bfloat16 [768, 8192], P('head', 'seq'), may hold values from -6 to 6
- values: bfloat16 [768, 8192], P('head', 'seq'), may hold values from -36 to 36
- slide_lengths: int32 [8], replicated, may hold values from 1 to 4096, 8192 in all
- norm_gain: float32 [768], P('head'), may hold values from 0.1 to 1.9
- norm_bias: float32 [768], P('head'), may hold values from -3 to 3
Outputs:
- encoded: bfloat16 [768, 8192], P('head', 'seq')
The draws below stay inside these ranges and needn't reach their ends.
Inputs may be any that keep to these rules, and one draw needn't show every extreme that they name: `slide_lengths`: positive slide lengths that sum to 8192; the longest is exactly 4096.
All inputs are finite; a program needn't handle non-finite values.
Results may differ from the reference program's by a relative error of at most 0.0041.
Values may be sent and summed in bfloat16 or wider, within the bound.
No kernel may reach another device: no remote copies, remote signals or barrier semaphores. Data moves between devices by JAX's collectives and lax.ppermute only.
A program may use at most 128 MiB of HBM per device.

```python
import math
import jax
import jax.numpy as jnp
import numpy as np
from jax import lax

D = 768
NH = 16
HD = 48
SEG = 1024
TOKENS = 8192
NSLIDES = 8
LONGEST = 4096


def draw_queries(key, part):
    base = jnp.clip(jax.random.normal(jax.random.fold_in(key, 1), (TOKENS, D), jnp.float32), -6.0, 6.0)
    return base.T.astype(jnp.bfloat16)


def draw_keys(key, part):
    base = jnp.clip(jax.random.normal(jax.random.fold_in(key, 2), (TOKENS, D), jnp.float32), -6.0, 6.0)
    return base.T.astype(jnp.bfloat16)


def draw_values(key, part):
    head_of = (jnp.arange(D) // HD).astype(jnp.float32)
    rising = jnp.exp(math.log(3.0) * head_of / (NH - 1))
    column = jnp.exp(jax.random.uniform(jax.random.fold_in(key, 5), (D,), minval=math.log(0.5), maxval=math.log(2.0)))
    base = jnp.clip(jax.random.normal(jax.random.fold_in(key, 6), (TOKENS, D), jnp.float32), -6.0, 6.0)
    return (base * rising[None, :] * column[None, :]).T.astype(jnp.bfloat16)


def levels(key, shape, cuts, smallest, high):
    level, own = 1.0, jax.random.fold_in(key, 6)
    for axis_at, shards_of in cuts:
        heights = jnp.exp(jax.random.uniform(jax.random.fold_in(own, axis_at), (shards_of,), jnp.float32, smallest / len(cuts), high / len(cuts)))
        level = level * jnp.repeat(heights, shape[axis_at] // shards_of).reshape([-1 if axis == axis_at else 1 for axis in range(len(shape))])
    return level


def profile(count, total, limit, skew):
    weights = [(1 << 20) // math.isqrt(rank ** skew) + 1 for rank in range(2, count + 1)]
    rest, holding = total - limit - (count - 1), [1] * (count - 1)
    while rest > 0:
        free = [i for i in range(count - 1) if holding[i] < limit]
        pool, budget = sum([weights[i] for i in free]), rest
        for i in free:
            addition = min(limit - holding[i], max(1, budget * weights[i] // pool), rest)
            holding[i] = holding[i] + addition
            rest = rest - addition
    return np.array([limit] + holding)


def uneven_parts(key, number_of, total, bound, lean):
    if number_of == 2:
        one = jax.random.randint(key, (), max(1, total - bound), min(bound, total - 1) + 1)
        return jnp.stack([one, total - one])
    lengths = jnp.asarray(profile(number_of, total, bound, lean), jnp.int32)
    pairs = (number_of - 1) // 2
    giver, sink = lengths[1:1 + 2 * pairs:2], lengths[2:2 + 2 * pairs:2]
    margin = jnp.minimum(giver - 1, bound - sink)
    moved = jax.random.randint(jax.random.fold_in(key, 1), (pairs,), 0, 1 << 20) % (margin + 1)
    lengths = lengths.at[1:1 + 2 * pairs:2].set(giver - moved).at[2:2 + 2 * pairs:2].set(sink + moved)
    return lengths[jax.random.permutation(jax.random.fold_in(key, 2), number_of)]


def noise(stream_key, dims, deviation, most, split=(), kind=jnp.bfloat16):
    values = deviation * jax.random.normal(stream_key, dims, jnp.float32)
    if split:
        values = values * levels(stream_key, dims, split, -0.22, 0.18)
    return jnp.clip(values, -most, most).astype(kind)


def setup_inputs(seed: int = 0) -> dict:
    arg_keys = jax.random.split(jax.random.key(seed), 7)
    queries = draw_queries(jax.random.fold_in(arg_keys[6], 71), 0)
    keys = draw_keys(jax.random.fold_in(arg_keys[6], 71), 0)
    values = draw_values(jax.random.fold_in(arg_keys[6], 71), 0)
    slide_lengths = uneven_parts(arg_keys[3], NSLIDES, TOKENS, LONGEST, 2).astype(jnp.int32)
    norm_gain = jnp.clip(1.0 + 0.18 * jax.random.normal(arg_keys[4], (D,), jnp.float32), 0.1, 1.9)
    norm_bias = noise(arg_keys[5], (D,), 0.5, 3.0, ((0, 4),), jnp.float32)
    return dict(queries=queries, keys=keys, values=values, slide_lengths=slide_lengths, norm_gain=norm_gain, norm_bias=norm_bias)


def slide_of(positions, slide_ends):
    return lax.optimization_barrier(jnp.sum((positions[..., None] >= slide_ends).astype(jnp.int32), axis=-1))

def attend_head(segment_items):
    query_rows, key_rows, value_rows, query_slide, key_slide = segment_items
    score_scale = 1.0 / math.sqrt(HD)
    scores = jnp.dot(query_rows, key_rows.T, preferred_element_type=jnp.float32) * score_scale
    scores = jnp.where(query_slide[:, None] == key_slide[None, :], scores, -1e+30)
    row_peak = lax.optimization_barrier(jnp.max(scores, axis=-1))
    probabilities = jnp.exp(scores - row_peak[:, None])
    totals = lax.optimization_barrier(jnp.sum(probabilities, axis=-1))
    weighted = jnp.dot(probabilities.astype(jnp.bfloat16), value_rows, preferred_element_type=jnp.float32)
    return (row_peak, totals, weighted)

def reference(queries, keys, values, slide_lengths, norm_gain, norm_bias):
    queries = queries.T
    keys = keys.T
    values = values.T
    slide_ends = jnp.cumsum(slide_lengths)

    def one_head(head_index):
        q_head = lax.dynamic_slice_in_dim(queries, head_index * HD, HD, 1)
        k_head = lax.dynamic_slice_in_dim(keys, head_index * HD, HD, 1)
        v_head = lax.dynamic_slice_in_dim(values, head_index * HD, HD, 1)
        running_peak = None
        weight = None
        accumulated = None
        for branch in range(4):
            dilation = 4 ** branch
            seg_span = min(SEG * dilation, TOKENS)
            seg_keys = seg_span // dilation
            compact_count = TOKENS // dilation
            offset = head_index % dilation

            def choose(matrix):
                shaped = matrix.reshape(compact_count, dilation, HD)
                return lax.dynamic_slice_in_dim(shaped, offset, 1, 1)[:, 0]
            compact_pos = dilation * jnp.arange(compact_count, dtype=jnp.int32) + offset
            compact_slide = slide_of(compact_pos, slide_ends)
            segment_count = TOKENS // seg_span
            items = (choose(q_head).reshape(segment_count, seg_keys, HD), choose(k_head).reshape(segment_count, seg_keys, HD), choose(v_head).reshape(segment_count, seg_keys, HD), compact_slide.reshape(segment_count, seg_keys), compact_slide.reshape(segment_count, seg_keys))
            row_peak, totals, weighted = lax.map(attend_head, items)
            row_peak = row_peak.reshape(compact_count)
            totals = totals.reshape(compact_count)
            weighted = weighted.reshape(compact_count, HD)
            chosen = jnp.arange(dilation, dtype=jnp.int32)[None, :] == offset
            peak_full = jnp.where(chosen, row_peak[:, None], jnp.float32(-1e+30)).reshape(TOKENS)
            total_full = jnp.where(chosen, totals[:, None], jnp.float32(0.0)).reshape(TOKENS)
            mixed_full = jnp.where(chosen[:, :, None], weighted[:, None, :], jnp.float32(0.0)).reshape(TOKENS, HD)
            if running_peak is None:
                running_peak, weight, accumulated = (peak_full, total_full, mixed_full)
            else:
                newest = jnp.maximum(running_peak, peak_full)
                keep_old = jnp.exp(running_peak - newest)
                keep_new = jnp.exp(peak_full - newest)
                weight = weight * keep_old + total_full * keep_new
                accumulated = accumulated * keep_old[:, None] + mixed_full * keep_new[:, None]
                running_peak = newest
        return accumulated / weight[:, None]
    per_head = lax.map(one_head, jnp.arange(NH, dtype=jnp.int32))
    attended = jnp.transpose(per_head, (1, 0, 2)).reshape(TOKENS, D)
    row_mean = lax.optimization_barrier(jnp.sum(attended, axis=1)) / D
    variance = lax.optimization_barrier(jnp.sum(attended * attended, axis=1)) / D - row_mean * row_mean
    normed = (attended - row_mean[:, None]) * lax.rsqrt(variance + 1e-05)[:, None]
    return (normed * norm_gain + norm_bias).astype(jnp.bfloat16).T
```

```python
import functools
import math

import jax
import jax.numpy as jnp
import numpy as np
from jax import lax
from jax.experimental import pallas as pl
from jax.experimental.pallas import tpu as pltpu
from jax.sharding import PartitionSpec as P

D = 768
HD = 48
SEG = 1024
HEADS = 4
BLOCKED = -1e30
SCALE = 1.0 / math.sqrt(HD)
LOG2_SCALE = math.log2(math.e) * SCALE
QUERY_CHUNK = 256
F32 = jnp.float32
BF16 = jnp.bfloat16
VMEM = pl.BlockSpec(memory_space=pltpu.VMEM)
SMEM = pl.BlockSpec(memory_space=pltpu.SMEM)
PARAMS = pltpu.CompilerParams(vmem_limit_bytes=40 * 2**20)


def partner(value, axis, mask):
    pairs = [(source, source ^ mask) for source in range(lax.axis_size(axis))]
    return lax.ppermute(value, axis, pairs)


def thirds(value):
    parts = []
    for _ in range(3):
        part = float(np.asarray(value, jnp.bfloat16))
        parts.append(part)
        value -= part
    return parts


def bias_rows(flags, factor):
    return [jnp.where(flags, F32(part), F32(0.0)) for part in thirds(math.log(factor) / SCALE)]


def flag_rows(flags):
    return [jnp.where(flags, F32(1.0), F32(0.0))] * 3


def slide_of(positions, lengths_ref):
    slide = jnp.zeros(positions.shape, jnp.int32)
    end = jnp.int32(0)
    for k in range(lengths_ref.shape[0]):
        end = end + lengths_ref[k]
        slide = slide + jnp.where(positions >= end, 1, 0)
    return slide


def stack_rows(rows, count):
    width = rows[0].shape[1]
    index = lax.broadcasted_iota(jnp.int32, (count, width), 0)
    block = jnp.zeros((count, width), F32)
    for k, row in enumerate(rows):
        block = jnp.where(index == k, row, block)
    return block


def lanes(width):
    return lax.broadcasted_iota(jnp.int32, (1, width), 1)


def compact_index(place, head_place):
    quarter = place >> 6
    return 16 * (place & 15) + 4 * ((place >> 4) & 3) + ((quarter + head_place) & 3)


def pack_kernel(k_ref, v_ref, quarter_ref, sixteenth_ref):
    rows = k_ref.shape[1]
    packed = rows // 4
    head_place = lax.axis_index("head")
    place = lax.broadcasted_iota(jnp.int32, (packed, rows), 0)
    group = lax.broadcasted_iota(jnp.int32, (packed, rows), 1) >> 2
    pick = jnp.where(compact_index(place, head_place) == group, F32(1.0), F32(0.0)).astype(BF16)
    own = lanes(rows) & 3
    results = []
    for ref in (k_ref, v_ref):
        masked = jnp.concatenate(
            [
                ref[i * HD : (i + 1) * HD, :]
                * jnp.broadcast_to(jnp.where(own == i, F32(1.0), F32(0.0)), (HD, rows)).astype(BF16)
                for i in range(HEADS)
            ],
            axis=0,
        )
        results.append(
            lax.dot_general(masked, pick, (((1,), (1,)), ((), ())), preferred_element_type=F32)
        )
    features = HEADS * HD
    quarter_ref[:features, :] = results[0].astype(BF16)
    quarter_ref[features:, :] = results[1].astype(BF16)
    few = packed // 4
    sixteenth_ref[...] = jnp.concatenate([results[0][:, :few], results[1][:, :few]], axis=1).astype(BF16)


def weigh(keys_t, queries, values):
    scores = jnp.dot(keys_t, queries, preferred_element_type=F32)
    peak = jnp.max(scores, axis=0, keepdims=True)
    probs = jnp.exp2((scores - peak) * LOG2_SCALE).astype(BF16)
    return peak, jnp.dot(values, probs, preferred_element_type=F32)


def local_kernel(first, lengths_ref, q_ref, k_ref, v_ref, out_ref):
    rows = q_ref.shape[1]
    slides = lengths_ref.shape[0]
    tile = lanes(rows)
    position = lax.axis_index("seq") * rows + tile
    head_place = lax.axis_index("head")
    slide = slide_of(position, lengths_ref)
    row = lax.broadcasted_iota(jnp.int32, (slides, rows), 0)
    same = slide == row
    query_slides = jnp.where(same, F32(1.0), F32(0.0))
    key_slides = jnp.where(same, F32(0.0), F32(BLOCKED))
    extra = -(-(slides + 9) // 16) * 16 - slides
    ones = jnp.ones((16, rows), BF16)
    for head in range(out_ref.shape[0]):
        i = first + head
        mine = slice(i * HD, (i + 1) * HD)
        second = (tile & 3) == i
        third = (tile & 15) == 4 * head_place + i
        fourth = (tile & 63) == 4 * head_place + i
        query_extra = stack_rows(flag_rows(second) + flag_rows(third) + flag_rows(fourth), extra)
        key_extra = stack_rows(
            bias_rows(second, 2.0) + bias_rows(third, 1.5) + bias_rows(fourth, 4.0 / 3.0), extra
        )
        queries = jnp.concatenate(
            [q_ref[mine, :], jnp.concatenate([query_slides, query_extra], axis=0).astype(BF16)], axis=0
        )
        keys = jnp.concatenate(
            [k_ref[mine, :], jnp.concatenate([key_slides, key_extra], axis=0).astype(BF16)], axis=0
        )
        keys_t = keys.T
        values = jnp.concatenate([v_ref[mine, :], ones], axis=0)
        for start in range(0, rows, QUERY_CHUNK):
            chunk = slice(start, start + QUERY_CHUNK)
            peak, mixed = weigh(keys_t, queries[:, chunk], values)
            out_ref[head, : HD + 8, chunk] = mixed[: HD + 8]
            out_ref[head, HD + 8 :, chunk] = jnp.broadcast_to(peak, (8, peak.shape[1]))


def distant_kernel(kinds, distances, lengths_ref, q_ref, local_a_ref, local_b_ref, *refs):
    pieces, (att_ref, sums_ref, k_ref, v_ref) = refs[: len(kinds)], refs[len(kinds) :]
    rows = q_ref.shape[1]
    features = HEADS * HD
    slides = lengths_ref.shape[0]
    tile = lanes(rows)
    seq_place = lax.axis_index("seq")
    head_place = lax.axis_index("head")
    extra = -(-(HEADS * slides + 8) // 16) * 16 - HEADS * slides

    at = 0
    spans = []
    for kind, distance, piece in zip(kinds, distances, pieces):
        count = rows // 4**kind
        place = lanes(count)
        group = compact_index(place, head_place)
        base = (seq_place ^ distance) * rows + 4 * group
        row = lax.broadcasted_iota(jnp.int32, (slides, count), 0)
        masks = [
            jnp.where(slide_of(base + i, lengths_ref) == row, F32(0.0), F32(BLOCKED))
            for i in range(HEADS)
        ]
        none = jnp.zeros((1, count), F32)
        always = none == 0.0
        in_third = place < rows // 16
        in_fourth = place < rows // 64
        if kind == 1:
            added = bias_rows(in_third, 2.0) + bias_rows(in_fourth, 1.5) + [none, none]
        elif kind == 2:
            added = [none] * 3 + bias_rows(in_fourth, 2.0) + [none + BLOCKED, none]
        else:
            added = [none] * 6 + [none, none + BLOCKED]
        masks.append(stack_rows(added, extra))
        mask_rows = jnp.concatenate(masks, axis=0).astype(BF16)
        if kind == 1:
            key_rows = piece[:features, :]
        else:
            key_rows = piece[:, :count]
        k_ref[at : at + count, :] = jnp.concatenate([key_rows, mask_rows], axis=0).T
        spans.append((at, count))
        at += count
    total_keys = at

    at = 0
    pending = []
    for kind, piece in zip(kinds, pieces):
        count = rows // 4**kind
        if kind == 1:
            v_ref[:features, at : at + count] = piece[features:, :]
            at += count
        else:
            half = rows // 16
            pending.append(piece[:, half : half + count])
            if sum(p.shape[1] for p in pending) == 256:
                v_ref[:features, at : at + 256] = jnp.concatenate(pending, axis=1)
                pending = []
                at += 256
    if pending:
        width = sum(p.shape[1] for p in pending)
        v_ref[:features, at : at + width] = jnp.concatenate(pending, axis=1)
    v_ref[features:, :] = jnp.ones((16, total_keys), BF16)

    slide = slide_of(seq_place * rows + tile, lengths_ref)
    row = lax.broadcasted_iota(jnp.int32, (slides, rows), 0)
    same = slide == row
    masks = [jnp.where(same & ((tile & 3) == i), F32(1.0), F32(0.0)) for i in range(HEADS)]
    third = ((tile >> 2) & 3) == head_place
    fourth = ((tile >> 2) & 15) == head_place
    masks.append(
        stack_rows(
            flag_rows(third) + flag_rows(fourth) + flag_rows(~third)[:1] + flag_rows(~fourth)[:1],
            extra,
        )
    )
    mask_rows = jnp.concatenate(masks, axis=0).astype(BF16)
    queries = jnp.concatenate(
        [
            q_ref[i * HD : (i + 1) * HD, :]
            * jnp.broadcast_to(jnp.where((tile & 3) == i, F32(1.0), F32(0.0)), (HD, rows)).astype(BF16)
            for i in range(HEADS)
        ]
        + [mask_rows],
        axis=0,
    )
    for start in range(0, rows, QUERY_CHUNK):
        chunk = slice(start, start + QUERY_CHUNK)
        peak, mixed = weigh(k_ref[...], queries[:, chunk], v_ref[...])
        total = mixed[features : features + 1]
        own = lanes(QUERY_CHUNK) & 3
        sums = squares = None
        for i in range(HEADS):
            ref = (local_a_ref, local_b_ref)[i // 2]
            selected = own == i
            here = ref[i % 2, HD + 8 : HD + 9, chunk]
            there = jnp.where(selected, peak, F32(BLOCKED))
            top = jnp.maximum(here, there)
            keep = jnp.exp2((here - top) * LOG2_SCALE)
            add = jnp.where(selected, jnp.exp2((there - top) * LOG2_SCALE), F32(0.0))
            inverse = 1.0 / (keep * ref[i % 2, HD : HD + 1, chunk] + add * total)
            attended = (
                ref[i % 2, :HD, chunk] * (keep * inverse)
                + mixed[i * HD : (i + 1) * HD] * (add * inverse)
            )
            att_ref[i * HD : (i + 1) * HD, chunk] = attended
            head_sum = jnp.sum(attended, axis=0, keepdims=True)
            head_squares = jnp.sum(attended * attended, axis=0, keepdims=True)
            sums = head_sum if sums is None else sums + head_sum
            squares = head_squares if squares is None else squares + head_squares
        at = start // QUERY_CHUNK
        sums_ref[at : at + 1, :] = sums
        sums_ref[4 + at : 5 + at, :] = squares


def norm_kernel(att_ref, gain_ref, bias_ref, *refs):
    sum_refs, out_ref = refs[:-1], refs[-1]
    features, rows = att_ref.shape
    r = lax.broadcasted_iota(jnp.int32, (features, features), 0)
    c = lax.broadcasted_iota(jnp.int32, (features, features), 1)
    columns = [
        jnp.sum(jnp.where(r == c, ref[...], 0.0), axis=1, keepdims=True)
        for ref in (gain_ref, bias_ref)
    ]
    sums = sum_refs[0][...]
    for ref in sum_refs[1:]:
        sums = sums + ref[...]
    mean = sums[:4] / D
    variance = sums[4:] / D - mean * mean
    inverse = lax.rsqrt(variance + 1e-05)
    for at in range(rows // QUERY_CHUNK):
        chunk = slice(at * QUERY_CHUNK, (at + 1) * QUERY_CHUNK)
        normed = (att_ref[:, chunk] - mean[at : at + 1]) * inverse[at : at + 1]
        out_ref[:, chunk] = (normed * columns[0] + columns[1]).astype(BF16)


def cost(flops, moved, exps=0):
    return pl.CostEstimate(flops=int(flops), bytes_accessed=int(moved), transcendentals=int(exps))


def per_device(queries, keys, values, slide_lengths, norm_gain, norm_bias):
    features, rows = queries.shape
    devices = lax.axis_size("seq")
    total_rows = rows * devices
    spans = [min(SEG * 4**b, total_rows) // rows for b in range(4)]

    quarter, sixteenth = pl.pallas_call(
        pack_kernel,
        out_shape=(
            jax.ShapeDtypeStruct((2 * features, rows // 4), BF16),
            jax.ShapeDtypeStruct((features, rows // 8), BF16),
        ),
        in_specs=[VMEM, VMEM],
        out_specs=(VMEM, VMEM),
        compiler_params=PARAMS,
        cost_estimate=cost(2 * 384 * 256 * 1024, 10**6),
        name="pack",
    )(keys, values)

    def local(first, *operands):
        return pl.pallas_call(
            functools.partial(local_kernel, first),
            out_shape=jax.ShapeDtypeStruct((2, HD + 16, rows), F32),
            in_specs=[SMEM, VMEM, VMEM, VMEM],
            out_specs=VMEM,
            compiler_params=PARAMS,
            cost_estimate=cost(2 * 2 * rows * rows * 512, 10**6, 2 * rows * rows),
            name="local",
        )(*operands)

    near = [(partner(quarter, "seq", m), m) for m in range(1, spans[1])]
    beyond = [
        (partner(sixteenth, "seq", m), m) for m in range(spans[2], spans[3], spans[2])
    ]
    beyond = beyond + [
        (partner(piece, "seq", m), m ^ d)
        for m in range(spans[1], spans[2], spans[1])
        for piece, d in [(sixteenth, 0)] + beyond
    ]
    local_a = local(0, slide_lengths, queries, keys, values)
    held, beyond_pieces = lax.optimization_barrier((queries, [piece for piece, _ in beyond]))
    beyond = [(piece, d) for piece, (_, d) in zip(beyond_pieces, beyond)]
    beyond = beyond + [
        (partner(piece, "seq", m), m ^ d) for m in range(1, spans[1]) for piece, d in beyond
    ]
    local_b = local(2, slide_lengths, held, keys, values)
    pieces = [(piece, d, 1) for piece, d in near]
    pieces += [(piece, d, 2 if d < spans[2] else 3) for piece, d in beyond]
    kinds = [kind for _, _, kind in pieces]
    distances = [d for _, d, _ in pieces]
    key_count = sum(rows // 4**kind for kind in kinds)
    depth = features + -(-(HEADS * slide_lengths.shape[0] + 8) // 16) * 16

    attended, sums = pl.pallas_call(
        functools.partial(distant_kernel, kinds, distances),
        out_shape=(
            jax.ShapeDtypeStruct((features, rows), F32),
            jax.ShapeDtypeStruct((8, rows // 4), F32),
        ),
        in_specs=[SMEM] + [VMEM] * (3 + len(pieces)),
        out_specs=(VMEM, VMEM),
        scratch_shapes=[
            pltpu.VMEM((key_count, depth), BF16),
            pltpu.VMEM((features + 16, key_count), BF16),
        ],
        compiler_params=PARAMS,
        cost_estimate=cost(2 * rows * key_count * 512, 10**6, rows * key_count),
        name="distant",
    )(slide_lengths, queries, local_a, local_b, *[piece for piece, _, _ in pieces])

    all_sums = [sums] + [partner(sums, "head", m) for m in range(1, lax.axis_size("head"))]
    return pl.pallas_call(
        norm_kernel,
        out_shape=jax.ShapeDtypeStruct((features, rows), BF16),
        in_specs=[VMEM] * (3 + len(all_sums)),
        out_specs=VMEM,
        compiler_params=PARAMS,
        name="norm",
    )(attended, norm_gain[None, :], norm_bias[None, :], *all_sums)


def solution(mesh):
    placed = (P("head", "seq"), P("head", "seq"), P("head", "seq"), P(), P("head"), P("head"))
    return jax.shard_map(
        per_device, mesh=mesh, in_specs=placed, out_specs=P("head", "seq"), check_vma=False
    )
```

```python
import functools
import math

import jax
import jax.numpy as jnp
import numpy as np
from jax import lax
from jax.experimental import pallas as pl
from jax.experimental.pallas import tpu as pltpu
from jax.sharding import PartitionSpec as P

D = 768
HD = 48
SEG = 1024
HEADS = 4
BLOCKED = -1e30
SCALE = 1.0 / math.sqrt(HD)
LOG2_SCALE = math.log2(math.e) * SCALE
QUERY_CHUNK = 1024
SAFE = 60.0
F32 = jnp.float32
BF16 = jnp.bfloat16
HBM = pl.BlockSpec(memory_space=pltpu.HBM)
VMEM = pl.BlockSpec(memory_space=pltpu.VMEM)
SMEM = pl.BlockSpec(memory_space=pltpu.SMEM)
PACK_LIMIT = 60 * 2**20
PARAMS = pltpu.CompilerParams(vmem_limit_bytes=40 * 2**20)


def partner(value, axis, mask):
    pairs = [(source, source ^ mask) for source in range(lax.axis_size(axis))]
    return lax.ppermute(value, axis, pairs)


def thirds(value):
    parts = []
    for _ in range(3):
        part = float(np.asarray(value, jnp.bfloat16))
        parts.append(part)
        value -= part
    return parts


def bias_rows(flags, factor):
    return [jnp.where(flags, F32(part), F32(0.0)) for part in thirds(math.log(factor) / SCALE)]


def flag_rows(flags):
    return [jnp.where(flags, F32(1.0), F32(0.0))] * 3


def slide_of(positions, lengths_ref):
    slide = jnp.zeros(positions.shape, jnp.int32)
    end = jnp.int32(0)
    for k in range(lengths_ref.shape[0]):
        end = end + lengths_ref[k]
        slide = slide + jnp.where(positions >= end, 1, 0)
    return slide


def stack_rows(rows, count):
    width = rows[0].shape[1]
    index = lax.broadcasted_iota(jnp.int32, (count, width), 0)
    block = jnp.zeros((count, width), F32)
    for k, row in enumerate(rows):
        block = jnp.where(index == k, row, block)
    return block


def lanes(width):
    return lax.broadcasted_iota(jnp.int32, (1, width), 1)


def compact_index(place, head_place):
    quarter = place >> 6
    return 16 * (place & 15) + 4 * ((place >> 4) & 3) + ((quarter + head_place) & 3)


def only_head(ref, own):
    width = ref.shape[1]
    return [
        ref[i * HD : (i + 1) * HD, :]
        * jnp.broadcast_to(jnp.where(own == i, F32(1.0), F32(0.0)), (HD, width)).astype(BF16)
        for i in range(HEADS)
    ]


def pack_kernel(k_hbm, v_hbm, pair_ref, sixteenth_ref, *scratch):
    targets, arrived = scratch[:2], scratch[2]
    copies = []
    for at, (source, target) in enumerate(zip((k_hbm, v_hbm), targets)):
        for i in range(HEADS):
            part = pl.ds(i * HD, HD)
            copies.append(
                pltpu.make_async_copy(source.at[part, :], target.at[part, :], arrived.at[at, i])
            )
    for copy in copies:
        copy.start()
    features, rows = targets[0].shape
    packed = rows // 4
    head_place = lax.axis_index("head")
    place = lax.broadcasted_iota(jnp.int32, (packed, rows), 0)
    group = lax.broadcasted_iota(jnp.int32, (packed, rows), 1) >> 2
    pick = jnp.where(compact_index(place, head_place) == group, F32(1.0), F32(0.0)).astype(BF16)
    own = lanes(rows) & 3
    results = []
    for at, ref in enumerate(targets):
        for copy in copies[at * HEADS : (at + 1) * HEADS]:
            copy.wait()
        masked = jnp.concatenate(only_head(ref, own), axis=0)
        compact = lax.dot_general(masked, pick, (((1,), (1,)), ((), ())), preferred_element_type=F32)
        pair_ref[at * features : (at + 1) * features, :] = compact.astype(BF16)
        results.append(compact[:, : packed // 4])
    sixteenth_ref[...] = jnp.concatenate(results, axis=1).astype(BF16)


def relay_kernel(one_ref, two_ref, *refs):
    beyond, (to_one, to_two) = refs[:-2], refs[-2:]
    features, width = to_one.shape[0], one_ref.shape[1]
    to_one[:, :width] = two_ref[features:, :]
    to_two[:, :width] = one_ref[:features, :]
    for piece in beyond:
        for out in (to_one, to_two):
            out[:, width : width + piece.shape[1]] = piece[...]
        width += piece.shape[1]


def mask_kernel(kinds, distances, lengths_ref, gain_ref, bias_ref, q_ref, q_out, k_mask_out, affine_out, q_norm_out, slide_out):
    rows = q_ref.shape[1]
    features = HEADS * HD
    slides = lengths_ref.shape[0]
    tile = lanes(rows)
    seq_place = lax.axis_index("seq")
    head_place = lax.axis_index("head")
    extra = k_mask_out.shape[0] - HEADS * slides

    at = 0
    for kind, distance in zip(kinds, distances):
        count = rows // 4**kind
        place = lanes(count)
        base = (seq_place ^ distance) * rows + 4 * compact_index(place, head_place)
        row = lax.broadcasted_iota(jnp.int32, (slides, count), 0)
        masks = [
            jnp.where(slide_of(base + i, lengths_ref) == row, F32(0.0), F32(BLOCKED))
            for i in range(HEADS)
        ]
        none = jnp.zeros((1, count), F32)
        in_third = place < rows // 16
        in_fourth = place < rows // 64
        if kind == 1:
            added = bias_rows(in_third, 2.0) + bias_rows(in_fourth, 1.5) + [none, none]
        elif kind == 2:
            added = [none] * 3 + bias_rows(in_fourth, 2.0) + [none + BLOCKED, none]
        else:
            added = [none] * 6 + [none, none + BLOCKED]
        masks.append(stack_rows(added, extra))
        k_mask_out[:, at : at + count] = jnp.concatenate(masks, axis=0).astype(BF16)
        at += count

    slide = slide_of(seq_place * rows + tile, lengths_ref)
    same = slide == lax.broadcasted_iota(jnp.int32, (slides, rows), 0)
    slide_out[...] = jnp.where(same, F32(1.0), F32(0.0))
    masks = [jnp.where(same & ((tile & 3) == i), F32(1.0), F32(0.0)) for i in range(HEADS)]
    third = ((tile >> 2) & 3) == head_place
    fourth = ((tile >> 2) & 15) == head_place
    masks.append(
        stack_rows(
            flag_rows(third) + flag_rows(fourth) + flag_rows(~third)[:1] + flag_rows(~fourth)[:1],
            extra,
        )
    )
    q_out[:features, :] = jnp.concatenate(only_head(q_ref, tile & 3), axis=0)
    q_out[features:, :] = jnp.concatenate(masks, axis=0).astype(BF16)

    q_norm_out[...] = jnp.full(q_norm_out.shape, largest_norm(q_ref[...]))

    r = lax.broadcasted_iota(jnp.int32, (features, features), 0)
    c = lax.broadcasted_iota(jnp.int32, (features, features), 1)
    for at, ref in enumerate((gain_ref, bias_ref)):
        column = jnp.sum(jnp.where(r == c, ref[...], 0.0), axis=1, keepdims=True)
        affine_out[at] = jnp.broadcast_to(column, (features, 128))


def largest_norm(rows):
    rows = rows.astype(F32)
    squares = rows * rows
    return functools.reduce(
        jnp.maximum,
        [jnp.max(jnp.sum(squares[i : i + HD], axis=0)) for i in range(0, rows.shape[0], HD)],
    )


def small(query_norm, key_norm):
    return query_norm * key_norm <= (SAFE / SCALE) ** 2


def weigh(keys_t, queries, values, find_peak):
    scores = jnp.dot(keys_t, queries, preferred_element_type=F32)
    if find_peak:
        peak = jnp.max(scores, axis=0, keepdims=True)
        scores = scores - peak
    else:
        peak = jnp.zeros((1, scores.shape[1]), F32)
    probs = jnp.exp2(scores * LOG2_SCALE).astype(BF16)
    return peak, jnp.dot(values, probs, preferred_element_type=F32)


def both_ways(safe, branch):
    pl.when(safe)(functools.partial(branch, False))
    pl.when(jnp.logical_not(safe))(functools.partial(branch, True))


def local_kernel(first, slide_ref, q_ref, k_ref, v_ref, out_ref):
    rows = q_ref.shape[1]
    slides = slide_ref.shape[0]
    heads = out_ref.shape[0]
    tile = lanes(rows)
    head_place = lax.axis_index("head")
    query_slides = slide_ref[...]
    key_slides = (1.0 - query_slides) * F32(BLOCKED)
    extra = -(-(slides + 9) // 16) * 16 - slides
    ones = jnp.ones((16, rows), BF16)
    all_mine = slice(first * HD, (first + heads) * HD)

    def branch(find_peak):
        for head in range(heads):
            i = first + head
            mine = slice(i * HD, (i + 1) * HD)
            second = (tile & 3) == i
            third = (tile & 15) == 4 * head_place + i
            fourth = (tile & 63) == 4 * head_place + i
            query_extra = stack_rows(flag_rows(second) + flag_rows(third) + flag_rows(fourth), extra)
            key_extra = stack_rows(
                bias_rows(second, 2.0) + bias_rows(third, 1.5) + bias_rows(fourth, 4.0 / 3.0), extra
            )
            queries = jnp.concatenate(
                [q_ref[mine, :], jnp.concatenate([query_slides, query_extra], axis=0).astype(BF16)],
                axis=0,
            )
            keys = jnp.concatenate(
                [k_ref[mine, :], jnp.concatenate([key_slides, key_extra], axis=0).astype(BF16)],
                axis=0,
            )
            keys_t = keys.T
            values = jnp.concatenate([v_ref[mine, :], ones], axis=0)
            for start in range(0, rows, QUERY_CHUNK):
                chunk = slice(start, start + QUERY_CHUNK)
                peak, mixed = weigh(keys_t, queries[:, chunk], values, find_peak)
                out_ref[head, : HD + 8, chunk] = mixed[: HD + 8]
                out_ref[head, HD + 8 :, chunk] = jnp.broadcast_to(peak, (8, peak.shape[1]))

    both_ways(small(largest_norm(q_ref[all_mine, :]), largest_norm(k_ref[all_mine, :])), branch)


def distant_parts(pieces, mask_at, q_norm_ref, q_ref, k_mask_ref, k_ref, v_ref, use):
    features = HEADS * HD
    rows = q_ref.shape[1]
    at = 0
    norms = []
    beside = []
    for kind, keys, values in pieces:
        count = rows // 4**kind
        key_rows = keys[:, :count]
        if kind == 1:
            v_ref[:features, at : at + count] = values[...]
        else:
            beside.append(values[:, rows // 16 : rows // 16 + count])
        norms.append(largest_norm(key_rows))
        masks = k_mask_ref[:, mask_at + at : mask_at + at + count]
        k_ref[at : at + count, :] = jnp.concatenate([key_rows, masks], axis=0).T
        at += count
    if beside:
        width = sum(part.shape[1] for part in beside)
        v_ref[:features, at - width : at] = jnp.concatenate(beside, axis=1)
    v_ref[features:, :] = jnp.ones((16, at), BF16)

    def branch(find_peak):
        use(*weigh(k_ref[...], q_ref[...], v_ref[...], find_peak))

    key_norm = functools.reduce(jnp.maximum, norms)
    both_ways(small(jnp.max(q_norm_ref[...]), key_norm), branch)


def halves(ref):
    features = HEADS * HD
    return ref.at[:features, :], ref.at[features:, :]


def near_kernel(q_norm_ref, q_ref, k_mask_ref, one_ref, two_ref, out_ref, k_ref, v_ref):
    features = HEADS * HD

    def use(peak, mixed):
        out_ref[: features + 8, :] = mixed[: features + 8]
        out_ref[features + 8 :, :] = jnp.broadcast_to(peak, (8, peak.shape[1]))

    pieces = [(1, *halves(one_ref)), (1, *halves(two_ref))]
    distant_parts(pieces, 0, q_norm_ref, q_ref, k_mask_ref, k_ref, v_ref, use)


def last_kernel(kinds, mask_at, q_norm_ref, q_ref, k_mask_ref, local_a, local_b, near_ref, *refs):
    att_ref, sums_ref, k_ref, v_ref = refs[-4:]
    features = HEADS * HD
    rows = q_ref.shape[1]
    (from_one, from_two), rest = refs[:2], refs[2:-4]
    width = rows // 4
    pieces = [(1, from_two.at[:, :width], from_one.at[:, :width])]
    beyond = [ref.at[:, at : at + rows // 8] for ref in (from_one, from_two)
              for at in range(width, ref.shape[1], rows // 8)] + list(rest)
    pieces += [(kind, ref, ref) for kind, ref in zip(kinds[1:], beyond)]

    def use(far_peak, far):
        own = lanes(rows) & 3
        near_peak = near_ref[features + 8 : features + 9, :]
        near_total = near_ref[features : features + 1, :]
        far_total = far[features : features + 1]
        sums = squares = None
        for i in range(HEADS):
            ref = (local_a, local_b)[i // 2].at[i % 2]
            mine = slice(i * HD, (i + 1) * HD)
            selected = own == i
            here = ref[HD + 8 : HD + 9, :]
            top = jnp.maximum(
                here, jnp.where(selected, jnp.maximum(near_peak, far_peak), F32(BLOCKED))
            )
            keep = jnp.exp2((here - top) * LOG2_SCALE)
            near_keep = jnp.where(selected, jnp.exp2((near_peak - top) * LOG2_SCALE), F32(0.0))
            far_keep = jnp.where(selected, jnp.exp2((far_peak - top) * LOG2_SCALE), F32(0.0))
            inverse = 1.0 / (
                keep * ref[HD : HD + 1, :] + near_keep * near_total + far_keep * far_total
            )
            attended = (
                ref[:HD, :] * (keep * inverse)
                + near_ref[mine, :] * (near_keep * inverse)
                + far[mine] * (far_keep * inverse)
            )
            att_ref[mine, :] = attended
            head_sum = jnp.sum(attended, axis=0, keepdims=True)
            head_squares = jnp.sum(attended * attended, axis=0, keepdims=True)
            sums = head_sum if sums is None else sums + head_sum
            squares = head_squares if squares is None else squares + head_squares
        quarter = rows // 4
        for at in range(4):
            sums_ref[at : at + 1, :] = sums[:, at * quarter : (at + 1) * quarter]
            sums_ref[4 + at : 5 + at, :] = squares[:, at * quarter : (at + 1) * quarter]

    distant_parts(pieces, mask_at, q_norm_ref, q_ref, k_mask_ref, k_ref, v_ref, use)


def norm_kernel(att_ref, affine_ref, *refs):
    sum_refs, out_ref = refs[:-1], refs[-1]
    sums = sum_refs[0][...]
    for ref in sum_refs[1:]:
        sums = sums + ref[...]
    mean = sums[:4] / D
    variance = sums[4:] / D - mean * mean
    inverse = lax.rsqrt(variance + 1e-05)
    width = affine_ref.shape[2]
    quarter = mean.shape[1]
    for start in range(0, att_ref.shape[1], width):
        at, first = start // quarter, start % quarter
        part = slice(first, first + width)
        normed = (att_ref[:, start : start + width] - mean[at : at + 1, part]) * inverse[at : at + 1, part]
        out_ref[:, start : start + width] = (normed * affine_ref[0] + affine_ref[1]).astype(BF16)


def cost(flops, moved, exps=0):
    return pl.CostEstimate(flops=int(flops), bytes_accessed=int(moved), transcendentals=int(exps))


def per_device(queries, keys, values, slide_lengths, norm_gain, norm_bias):
    features, rows = queries.shape
    total_rows = rows * lax.axis_size("seq")
    spans = [min(SEG * 4**b, total_rows) // rows for b in range(4)]
    assert spans[1] == 4 and features == HEADS * HD
    pair, own = pl.pallas_call(
        pack_kernel,
        out_shape=(
            jax.ShapeDtypeStruct((2 * features, rows // 4), BF16),
            jax.ShapeDtypeStruct((features, rows // 8), BF16),
        ),
        in_specs=[HBM] * 2,
        out_specs=(VMEM,) * 2,
        scratch_shapes=[
            pltpu.VMEM((features, rows), BF16),
            pltpu.VMEM((features, rows), BF16),
            pltpu.SemaphoreType.DMA((2, HEADS)),
        ],
        compiler_params=pltpu.CompilerParams(vmem_limit_bytes=PACK_LIMIT),
        cost_estimate=cost(2 * 384 * 256 * 1024, 10**6),
        name="pack",
    )(keys, values)

    beyond = [(partner(own, "seq", m), m) for m in range(spans[2], spans[3], spans[2])]
    beyond = beyond + [
        (partner(piece, "seq", m), m ^ d)
        for m in range(spans[1], spans[2], spans[1])
        for piece, d in [(own, 0)] + beyond
    ]
    one, two = partner(pair, "seq", 1), partner(pair, "seq", 2)
    beyond_pieces = [piece for piece, _ in beyond]
    relayed = jax.ShapeDtypeStruct((features, rows // 4 + rows // 8 * len(beyond)), BF16)
    to_one, to_two = pl.pallas_call(
        relay_kernel,
        out_shape=(relayed, relayed),
        in_specs=[VMEM] * (2 + len(beyond)),
        out_specs=(VMEM, VMEM),
        compiler_params=PARAMS,
        cost_estimate=cost(0, 10**6),
        name="relay",
    )(one, two, *beyond_pieces)
    from_one, from_two = partner(to_one, "seq", 1), partner(to_two, "seq", 2)
    from_three = [partner(piece, "seq", 3) for piece in beyond_pieces]
    beyond_distances = [d ^ m for m in (1, 2, 0, 3) for _, d in beyond]
    distances = [1, 2, 3] + beyond_distances
    kinds = [1, 1, 1] + [2 if d < spans[2] else 3 for d in beyond_distances]
    counts = [rows // 4**kind for kind in kinds]
    near_count, far_count = sum(counts[:2]), sum(counts[2:])

    mask_rows = -(-(HEADS * slide_lengths.shape[0] + 8) // 16) * 16
    depth = features + mask_rows
    own_queries, key_masks, affine, query_norm, slides = pl.pallas_call(
        functools.partial(mask_kernel, kinds, distances),
        out_shape=(
            jax.ShapeDtypeStruct((depth, rows), BF16),
            jax.ShapeDtypeStruct((mask_rows, near_count + far_count), BF16),
            jax.ShapeDtypeStruct((2, features, 128), F32),
            jax.ShapeDtypeStruct((8, 128), F32),
            jax.ShapeDtypeStruct((slide_lengths.shape[0], rows), F32),
        ),
        in_specs=[SMEM, VMEM, VMEM, VMEM],
        out_specs=(VMEM,) * 5,
        compiler_params=PARAMS,
        cost_estimate=cost(10**8, 10**6),
        name="masks",
    )(slide_lengths, norm_gain[None, :], norm_bias[None, :], queries)

    def local(first, *operands):
        return pl.pallas_call(
            functools.partial(local_kernel, first),
            out_shape=jax.ShapeDtypeStruct((2, HD + 16, rows), F32),
            in_specs=[VMEM] * 4,
            out_specs=VMEM,
            compiler_params=PARAMS,
            cost_estimate=cost(2 * 2 * rows * rows * 512, 10**6, 2 * rows * rows),
            name="local",
        )(*operands)

    local_a = local(0, slides, queries, keys, values)
    held, _ = lax.optimization_barrier((queries, (to_one, to_two)))
    local_b = local(2, slides, held, keys, values)

    def scratch(count):
        return [pltpu.VMEM((count, depth), BF16), pltpu.VMEM((features + 16, count), BF16)]

    near_part = pl.pallas_call(
        near_kernel,
        out_shape=jax.ShapeDtypeStruct((features + 16, rows), F32),
        in_specs=[VMEM] * 5,
        out_specs=VMEM,
        scratch_shapes=scratch(near_count),
        compiler_params=PARAMS,
        cost_estimate=cost(2 * rows * near_count * 512, 10**6, rows * near_count),
        name="near",
    )(query_norm, own_queries, key_masks, one, two)

    attended, sums = pl.pallas_call(
        functools.partial(last_kernel, kinds[2:], near_count),
        out_shape=(
            jax.ShapeDtypeStruct((features, rows), F32),
            jax.ShapeDtypeStruct((8, rows // 4), F32),
        ),
        in_specs=[VMEM] * (8 + 2 * len(beyond)),
        out_specs=(VMEM, VMEM),
        scratch_shapes=scratch(far_count),
        compiler_params=PARAMS,
        cost_estimate=cost(2 * rows * far_count * 512, 10**6, rows * far_count),
        name="last",
    )(
        query_norm, own_queries, key_masks, local_a, local_b, near_part,
        from_one, from_two, *beyond_pieces, *from_three,
    )

    all_sums = [sums] + [partner(sums, "head", m) for m in range(1, lax.axis_size("head"))]
    return pl.pallas_call(
        norm_kernel,
        out_shape=jax.ShapeDtypeStruct((features, rows), BF16),
        in_specs=[VMEM] * (2 + len(all_sums)),
        out_specs=VMEM,
        compiler_params=PARAMS,
        name="norm",
    )(attended, affine, *all_sums)


def solution(mesh):
    placed = (P("head", "seq"), P("head", "seq"), P("head", "seq"), P(), P("head"), P("head"))
    return jax.shard_map(
        per_device, mesh=mesh, in_specs=placed, out_specs=P("head", "seq"), check_vma=False
    )
```

```python
import functools
import math

import jax
import jax.numpy as jnp
import numpy as np
from jax import lax
from jax.experimental import pallas as pl
from jax.experimental.pallas import tpu as pltpu
from jax.sharding import PartitionSpec as P

D = 768
HD = 48
SEG = 1024
HEADS = 4
BLOCKED = -1e30
SCALE = 1.0 / math.sqrt(HD)
LOG2_SCALE = math.log2(math.e) * SCALE
LEAST, MOST = 1e-20, 1e30
F32 = jnp.float32
BF16 = jnp.bfloat16
HBM = pl.BlockSpec(memory_space=pltpu.HBM)
VMEM = pl.BlockSpec(memory_space=pltpu.VMEM)
SMEM = pl.BlockSpec(memory_space=pltpu.SMEM)
PACK_LIMIT = 107 * 2**19
PARAMS = pltpu.CompilerParams(vmem_limit_bytes=40 * 2**20)


def partner(value, axis, mask):
    pairs = [(source, source ^ mask) for source in range(lax.axis_size(axis))]
    return lax.ppermute(value, axis, pairs)


def thirds(value):
    parts = []
    for _ in range(3):
        part = float(np.asarray(value, jnp.bfloat16))
        parts.append(part)
        value -= part
    return parts


def bias_rows(flags, factor):
    return [jnp.where(flags, F32(part), F32(0.0)) for part in thirds(math.log(factor) / SCALE)]


def flag_rows(flags):
    return [jnp.where(flags, F32(1.0), F32(0.0))] * 3


def slide_of(positions, lengths_ref):
    slide = jnp.zeros(positions.shape, jnp.int32)
    end = jnp.int32(0)
    for k in range(lengths_ref.shape[0]):
        end = end + lengths_ref[k]
        slide = slide + jnp.where(positions >= end, 1, 0)
    return slide


def stack_rows(rows, count):
    width = rows[0].shape[1]
    index = lax.broadcasted_iota(jnp.int32, (count, width), 0)
    block = jnp.zeros((count, width), F32)
    for k, row in enumerate(rows):
        block = jnp.where(index == k, row, block)
    return block


def lanes(width):
    return lax.broadcasted_iota(jnp.int32, (1, width), 1)


def compact_index(place, head_place):
    quarter = place >> 6
    return 16 * (place & 15) + 4 * ((place >> 4) & 3) + ((quarter + head_place) & 3)


def only_head(ref, own):
    width = ref.shape[1]
    return [
        ref[i * HD : (i + 1) * HD, :]
        * jnp.broadcast_to(jnp.where(own == i, F32(1.0), F32(0.0)), (HD, width)).astype(BF16)
        for i in range(HEADS)
    ]


def pack_kernel(k_hbm, v_hbm, pair_ref, sixteenth_ref, *scratch):
    targets, arrived = scratch[:2], scratch[2]
    copies = []
    for at, (source, target) in enumerate(zip((k_hbm, v_hbm), targets)):
        for i in range(HEADS):
            part = pl.ds(i * HD, HD)
            copies.append(
                pltpu.make_async_copy(source.at[part, :], target.at[part, :], arrived.at[at, i])
            )
    for copy in copies:
        copy.start()
    features, rows = targets[0].shape
    packed = rows // 4
    head_place = lax.axis_index("head")
    group = lax.broadcasted_iota(jnp.int32, (rows, packed), 0) >> 2
    place = lax.broadcasted_iota(jnp.int32, (rows, packed), 1)
    pick = jnp.where(compact_index(place, head_place) == group, F32(1.0), F32(0.0)).astype(BF16)
    own = lanes(rows) & 3
    results = []
    for at, ref in enumerate(targets):
        for copy in copies[at * HEADS : (at + 1) * HEADS]:
            copy.wait()
        masked = jnp.concatenate(only_head(ref, own), axis=0)
        compact = jnp.dot(masked, pick, preferred_element_type=F32)
        pair_ref[at * features : (at + 1) * features, :] = compact.astype(BF16)
        results.append(compact[:, : packed // 4])
    sixteenth_ref[...] = jnp.concatenate(results, axis=1).astype(BF16)


def relay_kernel(one_ref, two_ref, *refs):
    beyond, (to_one, to_two) = refs[:-2], refs[-2:]
    features, width = to_one.shape[0], one_ref.shape[1]
    to_one[:, :width] = two_ref[features:, :]
    to_two[:, :width] = one_ref[:features, :]
    for at, piece in enumerate(beyond):
        count = piece.shape[1]
        for out, start in ((to_one, width), (to_two, width)):
            out[:, start + at * count : start + (at + 1) * count] = piece[...]


def pass_kernel(*refs):
    out = refs[-1]
    at = 0
    for piece in refs[:-1]:
        out[:, at : at + piece.shape[1]] = piece[...]
        at += piece.shape[1]


def mask_kernel(kinds, distances, lengths_ref, gain_ref, bias_ref, q_ref, q_out, k_mask_out, affine_out, slide_out):
    rows = q_ref.shape[1]
    features = HEADS * HD
    slides = lengths_ref.shape[0]
    tile = lanes(rows)
    seq_place = lax.axis_index("seq")
    head_place = lax.axis_index("head")
    extra = k_mask_out.shape[0] - HEADS * slides

    counts = [rows // 4**kind for kind in kinds]
    total = sum(counts)
    first = jnp.concatenate(
        [
            (seq_place ^ distance) * rows + 4 * compact_index(lanes(count), head_place)
            for count, distance in zip(counts, distances)
        ],
        axis=1,
    )
    slide = slide_of(first + lax.broadcasted_iota(jnp.int32, (HEADS, total), 0), lengths_ref)
    row = lax.broadcasted_iota(jnp.int32, (slides, total), 0)
    masks = [jnp.where(slide[i : i + 1] == row, F32(0.0), F32(BLOCKED)) for i in range(HEADS)]
    added = []
    for kind, count in zip(kinds, counts):
        place = lanes(count)
        none = jnp.zeros((1, count), F32)
        in_third = place < rows // 16
        in_fourth = place < rows // 64
        if kind == 1:
            extras = bias_rows(in_third, 2.0) + bias_rows(in_fourth, 1.5) + [none, none]
        elif kind == 2:
            extras = [none] * 3 + bias_rows(in_fourth, 2.0) + [none + BLOCKED, none]
        else:
            extras = [none] * 6 + [none, none + BLOCKED]
        added.append(stack_rows(extras, extra))
    masks.append(jnp.concatenate(added, axis=1))
    k_mask_out[...] = jnp.concatenate(masks, axis=0).astype(BF16)

    slide = slide_of(seq_place * rows + tile, lengths_ref)
    same = slide == lax.broadcasted_iota(jnp.int32, (slides, rows), 0)
    slide_out[...] = jnp.where(same, F32(1.0), F32(0.0))
    masks = [jnp.where(same & ((tile & 3) == i), F32(1.0), F32(0.0)) for i in range(HEADS)]
    third = ((tile >> 2) & 3) == head_place
    fourth = ((tile >> 2) & 15) == head_place
    masks.append(
        stack_rows(
            flag_rows(third) + flag_rows(fourth) + flag_rows(~third)[:1] + flag_rows(~fourth)[:1],
            extra,
        )
    )
    q_out[:features, :] = jnp.concatenate(only_head(q_ref, tile & 3), axis=0)
    q_out[features:, :] = jnp.concatenate(masks, axis=0).astype(BF16)

    r = lax.broadcasted_iota(jnp.int32, (features, features), 0)
    c = lax.broadcasted_iota(jnp.int32, (features, features), 1)
    for at, ref in enumerate((gain_ref, bias_ref)):
        column = jnp.sum(jnp.where(r == c, ref[...], 0.0), axis=1, keepdims=True)
        affine_out[at] = jnp.broadcast_to(column, (features, 128))


def weigh(keys_t, queries, values):
    scores = jnp.dot(keys_t, queries, preferred_element_type=F32)
    probs = jnp.exp2(scores * LOG2_SCALE).astype(BF16)
    return jnp.dot(values, probs, preferred_element_type=F32)


def weigh_with_peak(keys_t, queries, values):
    scores = jnp.dot(keys_t, queries, preferred_element_type=F32)
    peak = jnp.max(scores, axis=0, keepdims=True)
    probs = jnp.exp2((scores - peak) * LOG2_SCALE).astype(BF16)
    return peak, jnp.dot(values, probs, preferred_element_type=F32)


def local_operands(i, slide_ref, q_ref, k_ref, v_ref):
    rows = q_ref.shape[1]
    slides = slide_ref.shape[0]
    tile = lanes(rows)
    head_place = lax.axis_index("head")
    query_slides = slide_ref[...]
    key_slides = (1.0 - query_slides) * F32(BLOCKED)
    extra = -(-(slides + 9) // 16) * 16 - slides
    mine = slice(i * HD, (i + 1) * HD)
    second = (tile & 3) == i
    third = (tile & 15) == 4 * head_place + i
    fourth = (tile & 63) == 4 * head_place + i
    query_extra = stack_rows(flag_rows(second) + flag_rows(third) + flag_rows(fourth), extra)
    key_extra = stack_rows(
        bias_rows(second, 2.0) + bias_rows(third, 1.5) + bias_rows(fourth, 4.0 / 3.0), extra
    )
    queries = jnp.concatenate(
        [q_ref[mine, :], jnp.concatenate([query_slides, query_extra], axis=0).astype(BF16)], axis=0
    )
    keys = jnp.concatenate(
        [k_ref[mine, :], jnp.concatenate([key_slides, key_extra], axis=0).astype(BF16)], axis=0
    )
    values = jnp.concatenate([v_ref[mine, :], jnp.ones((16, rows), BF16)], axis=0)
    return keys.T, queries, values


def local_kernel(first, slide_ref, q_ref, k_ref, v_ref, out_ref):
    for head in range(out_ref.shape[0]):
        mixed = weigh(*local_operands(first + head, slide_ref, q_ref, k_ref, v_ref))
        out_ref[head] = mixed[: HD + 8]


def lay_out(pieces, mask_at, k_mask_ref, k_ref, v_ref):
    features = HEADS * HD
    at = 0
    beside = []
    for kind, keys, values in pieces:
        count = keys.shape[1] if kind == 1 else keys.shape[1] // 2 // 4 ** (kind - 2)
        if kind == 1:
            v_ref[:features, at : at + count] = values[...]
        else:
            half = values.shape[1] // 2
            beside.append(values[:, half : half + count])
        masks = k_mask_ref[:, mask_at + at : mask_at + at + count]
        k_ref[at : at + count, :] = jnp.concatenate([keys[:, :count], masks], axis=0).T
        at += count
    if beside:
        width = sum(part.shape[1] for part in beside)
        v_ref[:features, at - width : at] = jnp.concatenate(beside, axis=1)
    v_ref[features:, :at] = jnp.ones((16, at), BF16)


def halves(ref):
    features = HEADS * HD
    return ref.at[:features, :], ref.at[features:, :]


def with_more(i, part, total, mixed):
    features = HEADS * HD
    selected = (lanes(mixed.shape[1]) & 3) == i
    return (
        part + jnp.where(selected, mixed[i * HD : (i + 1) * HD], 0.0),
        total + jnp.where(selected, mixed[features : features + 1], 0.0),
    )


def parts_of(ref, i):
    features = HEADS * HD
    return ref[i * HD : (i + 1) * HD, :], ref[features + i : features + i + 1, :]


def store_parts(ref, i, part, total):
    features = HEADS * HD
    ref[i * HD : (i + 1) * HD, :] = part
    ref[features + i : features + i + 1, :] = total


def near_kernel(q_ref, k_mask_ref, local_a, local_b, one_ref, two_ref, out_ref, k_ref, v_ref):
    lay_out([(1, *halves(one_ref)), (1, *halves(two_ref))], 0, k_mask_ref, k_ref, v_ref)
    mixed = weigh(k_ref[...], q_ref[...], v_ref[...])
    for i in range(HEADS):
        ref = (local_a, local_b)[i // 2].at[i % 2]
        store_parts(out_ref, i, *with_more(i, ref[:HD, :], ref[HD : HD + 1, :], mixed))


def far_kernel(kinds, mask_at, q_ref, k_mask_ref, near_ref, *refs):
    out_ref, k_ref, v_ref = refs[-3:]
    pieces = far_pieces(kinds, q_ref.shape[1], *refs[:2], refs[2:-3])
    lay_out(pieces, mask_at, k_mask_ref, k_ref, v_ref)
    mixed = weigh(k_ref[...], q_ref[...], v_ref[...])
    for i in range(HEADS):
        store_parts(out_ref, i, *with_more(i, *parts_of(near_ref, i), mixed))


def far_pieces(kinds, rows, from_one, from_two, rest):
    width = rows // 4
    beyond = [
        ref.at[:, at : at + rows // 8]
        for ref in (from_one, from_two)
        for at in range(width, ref.shape[1], rows // 8)
    ] + list(rest)
    diagonal = (1, from_two.at[:, :width], from_one.at[:, :width])
    return [diagonal] + [(kind, ref, ref) for kind, ref in zip(kinds[1:], beyond)]


def three_pieces(kinds, rows, from_three):
    return [
        (kind, *[from_three.at[:, at * rows // 8 : (at + 1) * rows // 8]] * 2)
        for at, kind in enumerate(kinds)
    ]


def add_up(head_parts, att_ref, sums_ref):
    sums = squares = None
    for i, attended in enumerate(head_parts):
        att_ref[i * HD : (i + 1) * HD, :] = attended
        head_sum = jnp.sum(attended, axis=0, keepdims=True)
        head_squares = jnp.sum(attended * attended, axis=0, keepdims=True)
        sums = head_sum if sums is None else sums + head_sum
        squares = head_squares if squares is None else squares + head_squares
    quarter = sums_ref.shape[1]
    for at in range(4):
        sums_ref[at : at + 1, :] = sums[:, at * quarter : (at + 1) * quarter]
        sums_ref[4 + at : 5 + at, :] = squares[:, at * quarter : (at + 1) * quarter]


def last_kernel(kinds, mask_at, raw_refs, q_ref, k_mask_ref, far_ref, from_three, *refs):
    raw, (att_ref, sums_ref, k_three, v_three, k_ref, v_ref) = refs[:raw_refs], refs[raw_refs:]
    rows = q_ref.shape[1]
    features = HEADS * HD
    own = lanes(rows) & 3
    three = three_pieces(kinds[-(from_three.shape[1] * 8 // rows) :], rows, from_three)
    lay_out(three, mask_at, k_mask_ref, k_three, v_three)
    mixed = weigh(k_three[...], q_ref[...], v_three[...])
    parts = []
    least = most = None
    for i in range(HEADS):
        part, total = with_more(i, *parts_of(far_ref, i), mixed)
        parts.append(part * (1.0 / total))
        least = total if least is None else jnp.minimum(least, total)
        most = total if most is None else jnp.maximum(most, total)
    add_up(parts, att_ref, sums_ref)
    fine = (least >= LEAST) & (most <= MOST)
    worst = jnp.max(jnp.where(fine, 0.0, 1.0))

    @pl.when(worst > 0.0)
    def _():
        slide_ref, queries, keys, values, one_ref, two_ref, from_one, from_two = raw[:8]
        pieces = [(1, *halves(one_ref)), (1, *halves(two_ref))]
        pieces += far_pieces(kinds[2:], rows, from_one, from_two, raw[8:]) + three
        lay_out(pieces, 0, k_mask_ref, k_ref, v_ref)
        far_peak, mixed = weigh_with_peak(k_ref[...], q_ref[...], v_ref[...])
        parts = []
        for i in range(HEADS):
            mine = slice(i * HD, (i + 1) * HD)
            here, local = weigh_with_peak(*local_operands(i, slide_ref, queries, keys, values))
            there = jnp.where(own == i, far_peak, F32(BLOCKED))
            top = jnp.maximum(here, there)
            keep = jnp.exp2((here - top) * LOG2_SCALE)
            add = jnp.where(own == i, jnp.exp2((there - top) * LOG2_SCALE), F32(0.0))
            total = keep * local[HD : HD + 1] + add * mixed[features : features + 1]
            parts.append((local[:HD] * keep + mixed[mine] * add) / total)
        add_up(parts, att_ref, sums_ref)


def norm_kernel(att_ref, affine_ref, *refs):
    sum_refs, out_ref = refs[:-1], refs[-1]
    sums = sum_refs[0][...]
    for ref in sum_refs[1:]:
        sums = sums + ref[...]
    mean = sums[:4] / D
    variance = sums[4:] / D - mean * mean
    inverse = lax.rsqrt(variance + 1e-05)
    width = affine_ref.shape[2]
    quarter = mean.shape[1]
    for start in range(0, att_ref.shape[1], width):
        at, first = start // quarter, start % quarter
        part = slice(first, first + width)
        normed = (att_ref[:, start : start + width] - mean[at : at + 1, part]) * inverse[at : at + 1, part]
        out_ref[:, start : start + width] = (normed * affine_ref[0] + affine_ref[1]).astype(BF16)


def cost(flops, moved, exps=0):
    return pl.CostEstimate(flops=int(flops), bytes_accessed=int(moved), transcendentals=int(exps))


def per_device(queries, keys, values, slide_lengths, norm_gain, norm_bias):
    features, rows = queries.shape
    total_rows = rows * lax.axis_size("seq")
    spans = [min(SEG * 4**b, total_rows) // rows for b in range(4)]
    assert spans[1] == 4 and features == HEADS * HD
    pair, own = pl.pallas_call(
        pack_kernel,
        out_shape=(
            jax.ShapeDtypeStruct((2 * features, rows // 4), BF16),
            jax.ShapeDtypeStruct((features, rows // 8), BF16),
        ),
        in_specs=[HBM] * 2,
        out_specs=(VMEM,) * 2,
        scratch_shapes=[
            pltpu.VMEM((features, rows), BF16),
            pltpu.VMEM((features, rows), BF16),
            pltpu.SemaphoreType.DMA((2, HEADS)),
        ],
        compiler_params=pltpu.CompilerParams(vmem_limit_bytes=PACK_LIMIT),
        cost_estimate=cost(2 * 384 * 256 * 1024, 10**6),
        name="pack",
    )(keys, values)

    beyond = [(partner(own, "seq", m), m) for m in range(spans[2], spans[3], spans[2])]
    beyond = beyond + [
        (partner(piece, "seq", m), m ^ d)
        for m in range(spans[1], spans[2], spans[1])
        for piece, d in [(own, 0)] + beyond
    ]
    one, two = partner(pair, "seq", 1), partner(pair, "seq", 2)
    beyond_distances = [d ^ m for m in (1, 2, 0, 3) for _, d in beyond]
    distances = [1, 2, 3] + beyond_distances
    kinds = [1, 1, 1] + [2 if d < spans[2] else 3 for d in beyond_distances]
    counts = [rows // 4**kind for kind in kinds]
    three = len(kinds) - len(beyond)
    near_count, far_count, three_count = sum(counts[:2]), sum(counts[2:three]), sum(counts[three:])
    key_count = sum(counts)

    mask_rows = -(-(HEADS * slide_lengths.shape[0] + 8) // 16) * 16
    depth = features + mask_rows
    own_queries, key_masks, affine, slides = pl.pallas_call(
        functools.partial(mask_kernel, kinds, distances),
        out_shape=(
            jax.ShapeDtypeStruct((depth, rows), BF16),
            jax.ShapeDtypeStruct((mask_rows, key_count), BF16),
            jax.ShapeDtypeStruct((2, features, 128), F32),
            jax.ShapeDtypeStruct((slide_lengths.shape[0], rows), F32),
        ),
        in_specs=[SMEM, VMEM, VMEM, VMEM],
        out_specs=(VMEM,) * 4,
        compiler_params=PARAMS,
        cost_estimate=cost(10**8, 10**6),
        name="masks",
    )(slide_lengths, norm_gain[None, :], norm_bias[None, :], queries)

    def local(first, work, *operands):
        return pl.pallas_call(
            functools.partial(local_kernel, first),
            out_shape=jax.ShapeDtypeStruct((2, HD + 8, rows), F32),
            in_specs=[VMEM] * 4,
            out_specs=VMEM,
            compiler_params=PARAMS,
            cost_estimate=cost(work, 10**5),
            name="local",
        )(*operands)

    local_a = local(0, 10**9, slides, queries, keys, values)
    beyond_pieces = [piece for piece, _ in beyond]
    local_a, one, two, beyond_pieces = lax.optimization_barrier((local_a, one, two, beyond_pieces))
    relayed = jax.ShapeDtypeStruct((features, rows // 4 + rows // 8 * len(beyond)), BF16)
    passed_on = jax.ShapeDtypeStruct((features, rows // 8 * len(beyond)), BF16)
    to_one, to_two = pl.pallas_call(
        relay_kernel,
        out_shape=(relayed, relayed),
        in_specs=[VMEM] * (2 + len(beyond)),
        out_specs=(VMEM,) * 2,
        compiler_params=PARAMS,
        cost_estimate=cost(0, 10**6),
        name="relay",
    )(one, two, *beyond_pieces)
    from_one, from_two = partner(to_one, "seq", 1), partner(to_two, "seq", 2)
    to_three = pl.pallas_call(
        pass_kernel,
        out_shape=passed_on,
        in_specs=[VMEM] * len(beyond),
        out_specs=VMEM,
        compiler_params=PARAMS,
        cost_estimate=cost(0, 10**5),
        name="pass_on",
    )(*lax.optimization_barrier((beyond_pieces, to_one, to_two))[0])
    from_three = partner(to_three, "seq", 3)
    held, _ = lax.optimization_barrier((queries, (to_one, to_two, to_three)))
    local_b = local(2, 3 * 10**8, slides, held, keys, values)

    def scratch(count):
        return [pltpu.VMEM((count, depth), BF16), pltpu.VMEM((features + 16, count), BF16)]

    near_part = pl.pallas_call(
        near_kernel,
        out_shape=jax.ShapeDtypeStruct((features + 8, rows), F32),
        in_specs=[VMEM] * 6,
        out_specs=VMEM,
        scratch_shapes=scratch(near_count),
        compiler_params=PARAMS,
        cost_estimate=cost(2 * rows * near_count * 512, 10**5),
        name="near",
    )(own_queries, key_masks, local_a, local_b, one, two)

    far_part = pl.pallas_call(
        functools.partial(far_kernel, kinds[2:three], near_count),
        out_shape=jax.ShapeDtypeStruct((features + 8, rows), F32),
        in_specs=[VMEM] * (5 + len(beyond)),
        out_specs=VMEM,
        scratch_shapes=scratch(far_count),
        compiler_params=PARAMS,
        cost_estimate=cost(2 * rows * far_count * 512, 10**5),
        name="far",
    )(own_queries, key_masks, near_part, from_one, from_two, *beyond_pieces)

    raw = (slides, queries, keys, values, one, two, from_one, from_two, *beyond_pieces)
    attended, sums = pl.pallas_call(
        functools.partial(last_kernel, kinds, key_count - three_count, len(raw)),
        out_shape=(
            jax.ShapeDtypeStruct((features, rows), F32),
            jax.ShapeDtypeStruct((8, rows // 4), F32),
        ),
        in_specs=[VMEM] * (4 + len(raw)),
        out_specs=(VMEM, VMEM),
        scratch_shapes=scratch(three_count) + scratch(key_count),
        compiler_params=PARAMS,
        cost_estimate=cost(2 * rows * three_count * 512, 10**5),
        name="last",
    )(own_queries, key_masks, far_part, from_three, *raw)

    all_sums = [sums] + [partner(sums, "head", m) for m in range(1, lax.axis_size("head"))]
    return pl.pallas_call(
        norm_kernel,
        out_shape=jax.ShapeDtypeStruct((features, rows), BF16),
        in_specs=[VMEM] * (2 + len(all_sums)),
        out_specs=VMEM,
        compiler_params=PARAMS,
        name="norm",
    )(attended, affine, *all_sums)


def solution(mesh):
    placed = (P("head", "seq"), P("head", "seq"), P("head", "seq"), P(), P("head"), P("head"))
    return jax.shard_map(
        per_device, mesh=mesh, in_specs=placed, out_specs=P("head", "seq"), check_vma=False
    )
```

```python
import functools
import math

import jax
import jax.numpy as jnp
import numpy as np
from jax import lax
from jax.experimental import pallas as pl
from jax.experimental.pallas import tpu as pltpu
from jax.sharding import PartitionSpec as P

D = 768
HD = 48
SEG = 1024
HEADS = 4
BLOCKED = -1e30
SCALE = 1.0 / math.sqrt(HD)
LOG2_SCALE = math.log2(math.e) * SCALE
LEAST, MOST = 1e-20, 1e30
F32 = jnp.float32
BF16 = jnp.bfloat16
HBM = pl.BlockSpec(memory_space=pltpu.HBM)
VMEM = pl.BlockSpec(memory_space=pltpu.VMEM)
SMEM = pl.BlockSpec(memory_space=pltpu.SMEM)
PACK_LIMIT = 107 * 2**19
PARAMS = pltpu.CompilerParams(vmem_limit_bytes=40 * 2**20)


def partner(value, axis, mask):
    pairs = [(source, source ^ mask) for source in range(lax.axis_size(axis))]
    return lax.ppermute(value, axis, pairs)


def thirds(value):
    parts = []
    for _ in range(3):
        part = float(np.asarray(value, jnp.bfloat16))
        parts.append(part)
        value -= part
    return parts


def bias_rows(flags, factor):
    return [jnp.where(flags, F32(part), F32(0.0)) for part in thirds(math.log(factor) / SCALE)]


def flag_rows(flags):
    return [jnp.where(flags, F32(1.0), F32(0.0))] * 3


def slide_of(positions, lengths_ref):
    slide = jnp.zeros(positions.shape, jnp.int32)
    end = jnp.int32(0)
    for k in range(lengths_ref.shape[0]):
        end = end + lengths_ref[k]
        slide = slide + jnp.where(positions >= end, 1, 0)
    return slide


def stack_rows(rows, count):
    width = rows[0].shape[1]
    index = lax.broadcasted_iota(jnp.int32, (count, width), 0)
    block = jnp.zeros((count, width), F32)
    for k, row in enumerate(rows):
        block = jnp.where(index == k, row, block)
    return block


def lanes(width):
    return lax.broadcasted_iota(jnp.int32, (1, width), 1)


def compact_index(place, head_place):
    quarter = place >> 6
    return 16 * (place & 15) + 4 * ((place >> 4) & 3) + ((quarter + head_place) & 3)


def only_head(ref, own):
    width = ref.shape[1]
    return [
        ref[i * HD : (i + 1) * HD, :]
        * jnp.broadcast_to(jnp.where(own == i, F32(1.0), F32(0.0)), (HD, width)).astype(BF16)
        for i in range(HEADS)
    ]


def pack_kernel(k_hbm, v_hbm, pair_ref, sixteenth_ref, *scratch):
    targets, arrived = scratch[:2], scratch[2]
    copies = []
    for at, (source, target) in enumerate(zip((k_hbm, v_hbm), targets)):
        for i in range(HEADS):
            part = pl.ds(i * HD, HD)
            copies.append(
                pltpu.make_async_copy(source.at[part, :], target.at[part, :], arrived.at[at, i])
            )
    for copy in copies:
        copy.start()
    features, rows = targets[0].shape
    packed = rows // 4
    head_place = lax.axis_index("head")
    group = lax.broadcasted_iota(jnp.int32, (rows, packed), 0) >> 2
    place = lax.broadcasted_iota(jnp.int32, (rows, packed), 1)
    pick = jnp.where(compact_index(place, head_place) == group, F32(1.0), F32(0.0)).astype(BF16)
    own = lanes(rows) & 3
    results = []
    for at, ref in enumerate(targets):
        for copy in copies[at * HEADS : (at + 1) * HEADS]:
            copy.wait()
        masked = jnp.concatenate(only_head(ref, own), axis=0)
        compact = jnp.dot(masked, pick, preferred_element_type=F32)
        pair_ref[at * features : (at + 1) * features, :] = compact.astype(BF16)
        results.append(compact[:, : packed // 4])
    sixteenth_ref[...] = jnp.concatenate(results, axis=1).astype(BF16)


def relay_kernel(two_ref, to_one, to_two):
    half = to_two.shape[0]
    to_one[...] = two_ref[half:, :]
    to_two[...] = two_ref[:half, :]


def pass_kernel(*refs):
    out = refs[-1]
    at = 0
    for piece in refs[:-1]:
        out[:, at : at + piece.shape[1]] = piece[...]
        at += piece.shape[1]


def diagonal_pair(from_one, from_two):
    return from_two, from_one


def mask_kernel(kinds, distances, lengths_ref, gain_ref, bias_ref, q_ref, q_out, k_mask_out, affine_out, slide_out):
    rows = q_ref.shape[1]
    features = HEADS * HD
    slides = lengths_ref.shape[0]
    tile = lanes(rows)
    seq_place = lax.axis_index("seq")
    head_place = lax.axis_index("head")
    extra = k_mask_out.shape[0] - HEADS * slides

    counts = [rows // 4**kind for kind in kinds]
    total = sum(counts)
    first = jnp.concatenate(
        [
            (seq_place ^ distance) * rows + 4 * compact_index(lanes(count), head_place)
            for count, distance in zip(counts, distances)
        ],
        axis=1,
    )
    slide = slide_of(first + lax.broadcasted_iota(jnp.int32, (HEADS, total), 0), lengths_ref)
    row = lax.broadcasted_iota(jnp.int32, (slides, total), 0)
    masks = [jnp.where(slide[i : i + 1] == row, F32(0.0), F32(BLOCKED)) for i in range(HEADS)]
    added = []
    for kind, count in zip(kinds, counts):
        place = lanes(count)
        none = jnp.zeros((1, count), F32)
        in_third = place < rows // 16
        in_fourth = place < rows // 64
        if kind == 1:
            extras = bias_rows(in_third, 2.0) + bias_rows(in_fourth, 1.5) + [none, none]
        elif kind == 2:
            extras = [none] * 3 + bias_rows(in_fourth, 2.0) + [none + BLOCKED, none]
        else:
            extras = [none] * 6 + [none, none + BLOCKED]
        added.append(stack_rows(extras, extra))
    masks.append(jnp.concatenate(added, axis=1))
    k_mask_out[...] = jnp.concatenate(masks, axis=0).astype(BF16)

    slide = slide_of(seq_place * rows + tile, lengths_ref)
    same = slide == lax.broadcasted_iota(jnp.int32, (slides, rows), 0)
    slide_out[...] = jnp.where(same, F32(1.0), F32(0.0))
    masks = [jnp.where(same & ((tile & 3) == i), F32(1.0), F32(0.0)) for i in range(HEADS)]
    third = ((tile >> 2) & 3) == head_place
    fourth = ((tile >> 2) & 15) == head_place
    masks.append(
        stack_rows(
            flag_rows(third) + flag_rows(fourth) + flag_rows(~third)[:1] + flag_rows(~fourth)[:1],
            extra,
        )
    )
    q_out[:features, :] = jnp.concatenate(only_head(q_ref, tile & 3), axis=0)
    q_out[features:, :] = jnp.concatenate(masks, axis=0).astype(BF16)

    r = lax.broadcasted_iota(jnp.int32, (features, features), 0)
    c = lax.broadcasted_iota(jnp.int32, (features, features), 1)
    for at, ref in enumerate((gain_ref, bias_ref)):
        column = jnp.sum(jnp.where(r == c, ref[...], 0.0), axis=1, keepdims=True)
        affine_out[at] = jnp.broadcast_to(column, (features, 128))


def weigh(keys_t, queries, values):
    scores = jnp.dot(keys_t, queries, preferred_element_type=F32)
    probs = jnp.exp2(scores * LOG2_SCALE).astype(BF16)
    return jnp.dot(values, probs, preferred_element_type=F32)


def weigh_with_peak(keys_t, queries, values):
    scores = jnp.dot(keys_t, queries, preferred_element_type=F32)
    peak = jnp.max(scores, axis=0, keepdims=True)
    probs = jnp.exp2((scores - peak) * LOG2_SCALE).astype(BF16)
    return peak, jnp.dot(values, probs, preferred_element_type=F32)


def local_operands(i, slide_ref, q_ref, k_ref, v_ref):
    rows = q_ref.shape[1]
    slides = slide_ref.shape[0]
    tile = lanes(rows)
    head_place = lax.axis_index("head")
    query_slides = slide_ref[...]
    key_slides = (1.0 - query_slides) * F32(BLOCKED)
    extra = -(-(slides + 9) // 16) * 16 - slides
    mine = slice(i * HD, (i + 1) * HD)
    second = (tile & 3) == i
    third = (tile & 15) == 4 * head_place + i
    fourth = (tile & 63) == 4 * head_place + i
    query_extra = stack_rows(flag_rows(second) + flag_rows(third) + flag_rows(fourth), extra)
    key_extra = stack_rows(
        bias_rows(second, 2.0) + bias_rows(third, 1.5) + bias_rows(fourth, 4.0 / 3.0), extra
    )
    queries = jnp.concatenate(
        [q_ref[mine, :], jnp.concatenate([query_slides, query_extra], axis=0).astype(BF16)], axis=0
    )
    keys = jnp.concatenate(
        [k_ref[mine, :], jnp.concatenate([key_slides, key_extra], axis=0).astype(BF16)], axis=0
    )
    values = jnp.concatenate([v_ref[mine, :], jnp.ones((16, rows), BF16)], axis=0)
    return keys.T, queries, values


def local_kernel(first, slide_ref, q_ref, k_ref, v_ref, out_ref):
    for head in range(out_ref.shape[0]):
        mixed = weigh(*local_operands(first + head, slide_ref, q_ref, k_ref, v_ref))
        out_ref[head] = mixed[: HD + 8]


def count_of(kind, keys):
    return keys.shape[1] if kind == 1 else keys.shape[1] // 2 // 4 ** (kind - 2)


def with_masks(pieces, mask_at):
    placed = []
    for kind, keys, values in pieces:
        placed.append((kind, keys, values, mask_at))
        mask_at += count_of(kind, keys)
    return placed


def lay_out(pieces, k_mask_ref, k_ref, v_ref):
    features = HEADS * HD
    at = 0
    beside = []
    for kind, keys, values, mask_at in pieces:
        count = count_of(kind, keys)
        if kind == 1:
            v_ref[:features, at : at + count] = values[...]
        else:
            half = values.shape[1] // 2
            beside.append(values[:, half : half + count])
        masks = k_mask_ref[:, mask_at : mask_at + count]
        k_ref[at : at + count, :] = jnp.concatenate([keys[:, :count], masks], axis=0).T
        at += count
    if beside:
        width = sum(part.shape[1] for part in beside)
        v_ref[:features, at - width : at] = jnp.concatenate(beside, axis=1)
    v_ref[features:, :at] = jnp.ones((16, at), BF16)


def halves(ref):
    features = HEADS * HD
    return ref.at[:features, :], ref.at[features:, :]


def with_more(i, part, total, mixed):
    features = HEADS * HD
    selected = (lanes(mixed.shape[1]) & 3) == i
    return (
        part + jnp.where(selected, mixed[i * HD : (i + 1) * HD], 0.0),
        total + jnp.where(selected, mixed[features : features + 1], 0.0),
    )


def parts_of(ref, i):
    features = HEADS * HD
    return ref[i * HD : (i + 1) * HD, :], ref[features + i : features + i + 1, :]


def store_parts(ref, i, part, total):
    features = HEADS * HD
    ref[i * HD : (i + 1) * HD, :] = part
    ref[features + i : features + i + 1, :] = total


def near_pieces(kinds, one_ref, two_ref, direct):
    pieces = [(1, *halves(one_ref)), (1, *halves(two_ref))]
    return pieces + [(kind, ref, ref) for kind, ref in zip(kinds, direct)]


def last_pieces(kinds, from_one, from_two, from_beyond):
    width = from_one.shape[1] // 2
    passed_on = [from_beyond.at[:, at * width : (at + 1) * width] for at in range(len(kinds))]
    pieces = [(1, *diagonal_pair(from_one, from_two))]
    return pieces + [(kind, ref, ref) for kind, ref in zip(kinds, passed_on)]


def near_kernel(kinds, q_ref, k_mask_ref, local_a, local_c, local_d, one_ref, two_ref, *refs):
    direct, (out_ref, k_ref, v_ref) = refs[:-3], refs[-3:]
    pieces = with_masks(near_pieces(kinds, one_ref, two_ref, direct), 0)
    lay_out(pieces, k_mask_ref, k_ref, v_ref)
    mixed = weigh(k_ref[...], q_ref[...], v_ref[...])
    for i in range(HEADS):
        ref = [ref.at[j] for ref in (local_a, local_c, local_d) for j in range(ref.shape[0])][i]
        store_parts(out_ref, i, *with_more(i, ref[:HD, :], ref[HD : HD + 1, :], mixed))


def add_up(head_parts, att_ref, sums_ref):
    sums = squares = None
    for i, attended in enumerate(head_parts):
        att_ref[i * HD : (i + 1) * HD, :] = attended
        head_sum = jnp.sum(attended, axis=0, keepdims=True)
        head_squares = jnp.sum(attended * attended, axis=0, keepdims=True)
        sums = head_sum if sums is None else sums + head_sum
        squares = head_squares if squares is None else squares + head_squares
    quarter = sums_ref.shape[1]
    for at in range(4):
        sums_ref[at : at + 1, :] = sums[:, at * quarter : (at + 1) * quarter]
        sums_ref[4 + at : 5 + at, :] = squares[:, at * quarter : (at + 1) * quarter]


def last_kernel(kinds, raw_refs, q_ref, k_mask_ref, near_ref, from_one, from_two, from_beyond, *refs):
    raw, (att_ref, sums_ref, k_last, v_last, k_ref, v_ref) = refs[:raw_refs], refs[raw_refs:]
    features = HEADS * HD
    own = lanes(q_ref.shape[1]) & 3
    last = last_pieces(kinds, from_one, from_two, from_beyond)
    last = with_masks(last, k_ref.shape[0] - k_last.shape[0])
    lay_out(last, k_mask_ref, k_last, v_last)
    mixed = weigh(k_last[...], q_ref[...], v_last[...])
    parts = []
    least = most = None
    for i in range(HEADS):
        part, total = with_more(i, *parts_of(near_ref, i), mixed)
        parts.append(part * (1.0 / total))
        least = total if least is None else jnp.minimum(least, total)
        most = total if most is None else jnp.maximum(most, total)
    add_up(parts, att_ref, sums_ref)
    fine = (least >= LEAST) & (most <= MOST)
    worst = jnp.max(jnp.where(fine, 0.0, 1.0))

    @pl.when(worst > 0.0)
    def _():
        slide_ref, queries, keys, values, one_ref, two_ref = raw[:6]
        pieces = with_masks(near_pieces(kinds, one_ref, two_ref, raw[6:]), 0) + last
        pieces.sort(key=lambda piece: piece[0] > 1)
        lay_out(pieces, k_mask_ref, k_ref, v_ref)
        far_peak, mixed = weigh_with_peak(k_ref[...], q_ref[...], v_ref[...])
        parts = []
        for i in range(HEADS):
            mine = slice(i * HD, (i + 1) * HD)
            here, local = weigh_with_peak(*local_operands(i, slide_ref, queries, keys, values))
            there = jnp.where(own == i, far_peak, F32(BLOCKED))
            top = jnp.maximum(here, there)
            keep = jnp.exp2((here - top) * LOG2_SCALE)
            add = jnp.where(own == i, jnp.exp2((there - top) * LOG2_SCALE), F32(0.0))
            total = keep * local[HD : HD + 1] + add * mixed[features : features + 1]
            parts.append((local[:HD] * keep + mixed[mine] * add) / total)
        add_up(parts, att_ref, sums_ref)


def norm_kernel(att_ref, affine_ref, *refs):
    sum_refs, out_ref = refs[:-1], refs[-1]
    sums = sum_refs[0][...]
    for ref in sum_refs[1:]:
        sums = sums + ref[...]
    mean = sums[:4] / D
    variance = sums[4:] / D - mean * mean
    inverse = lax.rsqrt(variance + 1e-05)
    width = affine_ref.shape[2]
    quarter = mean.shape[1]
    for start in range(0, att_ref.shape[1], width):
        at, first = start // quarter, start % quarter
        part = slice(first, first + width)
        normed = (att_ref[:, start : start + width] - mean[at : at + 1, part]) * inverse[at : at + 1, part]
        out_ref[:, start : start + width] = (normed * affine_ref[0] + affine_ref[1]).astype(BF16)


def cost(flops, moved, exps=0):
    return pl.CostEstimate(flops=int(flops), bytes_accessed=int(moved), transcendentals=int(exps))


def per_device(queries, keys, values, slide_lengths, norm_gain, norm_bias):
    features, rows = queries.shape
    total_rows = rows * lax.axis_size("seq")
    spans = [min(SEG * 4**b, total_rows) // rows for b in range(4)]
    assert spans[1] == 4 and features == HEADS * HD
    pair, own = pl.pallas_call(
        pack_kernel,
        out_shape=(
            jax.ShapeDtypeStruct((2 * features, rows // 4), BF16),
            jax.ShapeDtypeStruct((features, rows // 8), BF16),
        ),
        in_specs=[HBM] * 2,
        out_specs=(VMEM,) * 2,
        scratch_shapes=[
            pltpu.VMEM((features, rows), BF16),
            pltpu.VMEM((features, rows), BF16),
            pltpu.SemaphoreType.DMA((2, HEADS)),
        ],
        compiler_params=pltpu.CompilerParams(vmem_limit_bytes=PACK_LIMIT),
        cost_estimate=cost(2 * 384 * 256 * 1024, 10**6),
        name="pack",
    )(keys, values)

    one, two = partner(pair, "seq", 1), partner(pair, "seq", 2)
    held = [(own, 0)]
    held += [(partner(own, "seq", m), m) for m in range(spans[2], spans[3], spans[2])]
    beyond = held[1:] + [
        (partner(piece, "seq", m ^ side), m ^ side ^ d)
        for m in range(0, spans[2], spans[1])
        for side in (0, 1)
        for piece, d in (held if m else held[1:] * side)
    ]
    beyond_kinds = [2 if d < spans[2] else 3 for _, d in beyond]
    kinds = [1, 1] + beyond_kinds + [1] + beyond_kinds
    distances = [1, 2] + [d for _, d in beyond] + [3] + [2 ^ d for _, d in beyond]
    counts = [rows // 4**kind for kind in kinds]
    key_count = sum(counts)
    near_count = (key_count + counts[0]) // 2
    last_count = key_count - near_count

    mask_rows = -(-(HEADS * slide_lengths.shape[0] + 8) // 16) * 16
    depth = features + mask_rows
    own_queries, key_masks, affine, slides = pl.pallas_call(
        functools.partial(mask_kernel, kinds, distances),
        out_shape=(
            jax.ShapeDtypeStruct((depth, rows), BF16),
            jax.ShapeDtypeStruct((mask_rows, key_count), BF16),
            jax.ShapeDtypeStruct((2, features, 128), F32),
            jax.ShapeDtypeStruct((slide_lengths.shape[0], rows), F32),
        ),
        in_specs=[SMEM, VMEM, VMEM, VMEM],
        out_specs=(VMEM,) * 4,
        compiler_params=PARAMS,
        cost_estimate=cost(10**8, 10**6),
        name="masks",
    )(slide_lengths, norm_gain[None, :], norm_bias[None, :], queries)

    def local(first, count, work, *operands):
        return pl.pallas_call(
            functools.partial(local_kernel, first),
            out_shape=jax.ShapeDtypeStruct((count, HD + 8, rows), F32),
            in_specs=[VMEM] * 4,
            out_specs=VMEM,
            compiler_params=PARAMS,
            cost_estimate=cost(work, 10**3),
            name="local",
        )(*operands)

    local_a = local(0, 1, 10**9, slides, queries, keys, values)
    beyond_pieces = [piece for piece, _ in beyond]
    local_a, two = lax.optimization_barrier((local_a, two))
    to_one, to_two = pl.pallas_call(
        relay_kernel,
        out_shape=(
            jax.ShapeDtypeStruct((features, rows // 4), BF16),
            jax.ShapeDtypeStruct((features, rows // 4), BF16),
        ),
        in_specs=[VMEM],
        out_specs=(VMEM,) * 2,
        compiler_params=PARAMS,
        cost_estimate=cost(0, 10**6),
        name="relay",
    )(two)
    from_one, from_two = partner(to_one, "seq", 1), partner(to_two, "seq", 1)
    held, _ = lax.optimization_barrier((queries, (to_one, to_two)))
    local_c = local(1, 1, 10**6, slides, held, keys, values)
    beyond_pieces, local_c = lax.optimization_barrier((beyond_pieces, local_c))
    to_beyond = pl.pallas_call(
        pass_kernel,
        out_shape=jax.ShapeDtypeStruct((features, rows // 8 * len(beyond)), BF16),
        in_specs=[VMEM] * len(beyond),
        out_specs=VMEM,
        compiler_params=PARAMS,
        cost_estimate=cost(0, 10**5),
        name="pass_on",
    )(*beyond_pieces)
    from_beyond = partner(to_beyond, "seq", 2)
    held, _ = lax.optimization_barrier((queries, to_beyond))
    local_d = local(2, 2, 10**6, slides, held, keys, values)

    def scratch(count):
        return [pltpu.VMEM((count, depth), BF16), pltpu.VMEM((features + 16, count), BF16)]

    near_part = pl.pallas_call(
        functools.partial(near_kernel, beyond_kinds),
        out_shape=jax.ShapeDtypeStruct((features + 8, rows), F32),
        in_specs=[VMEM] * (7 + len(beyond)),
        out_specs=VMEM,
        scratch_shapes=scratch(near_count),
        compiler_params=PARAMS,
        cost_estimate=cost(10**6, 10**4),
        name="near",
    )(own_queries, key_masks, local_a, local_c, local_d, one, two, *beyond_pieces)

    raw = (slides, queries, keys, values, one, two, *beyond_pieces)
    attended, sums = pl.pallas_call(
        functools.partial(last_kernel, beyond_kinds, len(raw)),
        out_shape=(
            jax.ShapeDtypeStruct((features, rows), F32),
            jax.ShapeDtypeStruct((8, rows // 4), F32),
        ),
        in_specs=[VMEM] * (6 + len(raw)),
        out_specs=(VMEM, VMEM),
        scratch_shapes=scratch(last_count) + scratch(key_count),
        compiler_params=PARAMS,
        cost_estimate=cost(2 * rows * last_count * 512, 10**5),
        name="last",
    )(own_queries, key_masks, near_part, from_one, from_two, from_beyond, *raw)

    all_sums = [sums] + [partner(sums, "head", m) for m in range(1, lax.axis_size("head"))]
    return pl.pallas_call(
        norm_kernel,
        out_shape=jax.ShapeDtypeStruct((features, rows), BF16),
        in_specs=[VMEM] * (2 + len(all_sums)),
        out_specs=VMEM,
        compiler_params=PARAMS,
        name="norm",
    )(attended, affine, *all_sums)


def solution(mesh):
    placed = (P("head", "seq"), P("head", "seq"), P("head", "seq"), P(), P("head"), P("head"))
    return jax.shard_map(
        per_device, mesh=mesh, in_specs=placed, out_specs=P("head", "seq"), check_vma=False
    )
```

```python
import functools
import math

import jax
import jax.numpy as jnp
import numpy as np
from jax import lax
from jax.experimental import pallas as pl
from jax.experimental.pallas import tpu as pltpu
from jax.sharding import PartitionSpec as P

D = 768
HD = 48
SEG = 1024
HEADS = 4
BLOCKED = -1e30
SCALE = 1.0 / math.sqrt(HD)
LOG2_SCALE = math.log2(math.e) * SCALE
LEAST, MOST = 1e-20, 1e30
F32 = jnp.float32
BF16 = jnp.bfloat16
HBM = pl.BlockSpec(memory_space=pltpu.HBM)
VMEM = pl.BlockSpec(memory_space=pltpu.VMEM)
SMEM = pl.BlockSpec(memory_space=pltpu.SMEM)
PACK_LIMIT = 107 * 2**19
PARAMS = pltpu.CompilerParams(vmem_limit_bytes=40 * 2**20)


def partner(value, axis, mask):
    pairs = [(source, source ^ mask) for source in range(lax.axis_size(axis))]
    return lax.ppermute(value, axis, pairs)


def thirds(value):
    parts = []
    for _ in range(3):
        part = float(np.asarray(value, jnp.bfloat16))
        parts.append(part)
        value -= part
    return parts


def bias_rows(flags, factor):
    return [jnp.where(flags, F32(part), F32(0.0)) for part in thirds(math.log(factor) / SCALE)]


def flag_rows(flags):
    return [jnp.where(flags, F32(1.0), F32(0.0))] * 3


def slide_of(positions, lengths_ref):
    slide = jnp.zeros(positions.shape, jnp.int32)
    end = jnp.int32(0)
    for k in range(lengths_ref.shape[0]):
        end = end + lengths_ref[k]
        slide = slide + jnp.where(positions >= end, 1, 0)
    return slide


def stack_rows(rows, count):
    width = rows[0].shape[1]
    index = lax.broadcasted_iota(jnp.int32, (count, width), 0)
    block = jnp.zeros((count, width), F32)
    for k, row in enumerate(rows):
        block = jnp.where(index == k, row, block)
    return block


def lanes(width):
    return lax.broadcasted_iota(jnp.int32, (1, width), 1)


def compact_index(place, head_place):
    quarter = place >> 6
    return 16 * (place & 15) + 4 * ((place >> 4) & 3) + ((quarter + head_place) & 3)


def only_head(ref, own):
    width = ref.shape[1]
    return [
        ref[i * HD : (i + 1) * HD, :]
        * jnp.broadcast_to(jnp.where(own == i, F32(1.0), F32(0.0)), (HD, width)).astype(BF16)
        for i in range(HEADS)
    ]


def pack_kernel(k_hbm, v_hbm, pair_ref, sixteenth_ref, *scratch):
    targets, arrived = scratch[:2], scratch[2]
    copies = []
    for at, (source, target) in enumerate(zip((k_hbm, v_hbm), targets)):
        for i in range(HEADS):
            part = pl.ds(i * HD, HD)
            copies.append(
                pltpu.make_async_copy(source.at[part, :], target.at[part, :], arrived.at[at, i])
            )
    for copy in copies:
        copy.start()
    features, rows = targets[0].shape
    packed = rows // 4
    head_place = lax.axis_index("head")
    group = lax.broadcasted_iota(jnp.int32, (rows, packed), 0) >> 2
    place = lax.broadcasted_iota(jnp.int32, (rows, packed), 1)
    pick = jnp.where(compact_index(place, head_place) == group, F32(1.0), F32(0.0)).astype(BF16)
    own = lanes(rows) & 3
    results = []
    for at, ref in enumerate(targets):
        for copy in copies[at * HEADS : (at + 1) * HEADS]:
            copy.wait()
        masked = jnp.concatenate(only_head(ref, own), axis=0)
        compact = jnp.dot(masked, pick, preferred_element_type=F32)
        pair_ref[at * features : (at + 1) * features, :] = compact.astype(BF16)
        results.append(compact[:, : packed // 4])
    sixteenth_ref[...] = jnp.concatenate(results, axis=1).astype(BF16)


def relay_kernel(two_ref, to_one, to_two):
    half = to_two.shape[0]
    to_one[...] = two_ref[half:, :]
    to_two[...] = two_ref[:half, :]


def pass_kernel(*refs):
    out = refs[-1]
    at = 0
    for piece in refs[:-1]:
        out[:, at : at + piece.shape[1]] = piece[...]
        at += piece.shape[1]


def diagonal_pair(from_one, from_two):
    return from_two, from_one


def mask_kernel(kinds, distances, lengths_ref, gain_ref, bias_ref, q_ref, q_out, k_mask_out, affine_out, slide_out):
    rows = q_ref.shape[1]
    features = HEADS * HD
    slides = lengths_ref.shape[0]
    tile = lanes(rows)
    seq_place = lax.axis_index("seq")
    head_place = lax.axis_index("head")
    extra = k_mask_out.shape[0] - HEADS * slides

    counts = [rows // 4**kind for kind in kinds]
    total = sum(counts)
    first = jnp.concatenate(
        [
            (seq_place ^ distance) * rows + 4 * compact_index(lanes(count), head_place)
            for count, distance in zip(counts, distances)
        ],
        axis=1,
    )
    slide = slide_of(first + lax.broadcasted_iota(jnp.int32, (HEADS, total), 0), lengths_ref)
    row = lax.broadcasted_iota(jnp.int32, (slides, total), 0)
    masks = [jnp.where(slide[i : i + 1] == row, F32(0.0), F32(BLOCKED)) for i in range(HEADS)]
    added = []
    for kind, count in zip(kinds, counts):
        place = lanes(count)
        none = jnp.zeros((1, count), F32)
        in_third = place < rows // 16
        in_fourth = place < rows // 64
        if kind == 1:
            extras = bias_rows(in_third, 2.0) + bias_rows(in_fourth, 1.5) + [none, none]
        elif kind == 2:
            extras = [none] * 3 + bias_rows(in_fourth, 2.0) + [none + BLOCKED, none]
        else:
            extras = [none] * 6 + [none, none + BLOCKED]
        added.append(stack_rows(extras, extra))
    masks.append(jnp.concatenate(added, axis=1))
    k_mask_out[...] = jnp.concatenate(masks, axis=0).astype(BF16)

    slide = slide_of(seq_place * rows + tile, lengths_ref)
    same = slide == lax.broadcasted_iota(jnp.int32, (slides, rows), 0)
    slide_out[...] = jnp.where(same, F32(1.0), F32(0.0))
    masks = [jnp.where(same & ((tile & 3) == i), F32(1.0), F32(0.0)) for i in range(HEADS)]
    third = ((tile >> 2) & 3) == head_place
    fourth = ((tile >> 2) & 15) == head_place
    masks.append(
        stack_rows(
            flag_rows(third) + flag_rows(fourth) + flag_rows(~third)[:1] + flag_rows(~fourth)[:1],
            extra,
        )
    )
    q_out[:features, :] = jnp.concatenate(only_head(q_ref, tile & 3), axis=0)
    q_out[features:, :] = jnp.concatenate(masks, axis=0).astype(BF16)

    r = lax.broadcasted_iota(jnp.int32, (features, features), 0)
    c = lax.broadcasted_iota(jnp.int32, (features, features), 1)
    for at, ref in enumerate((gain_ref, bias_ref)):
        column = jnp.sum(jnp.where(r == c, ref[...], 0.0), axis=1, keepdims=True)
        affine_out[at] = jnp.broadcast_to(column, (features, 128))


def weigh(keys_t, queries, values):
    scores = jnp.dot(keys_t, queries, preferred_element_type=F32)
    probs = jnp.exp2(scores * LOG2_SCALE).astype(BF16)
    return jnp.dot(values, probs, preferred_element_type=F32)


def weigh_with_peak(keys_t, queries, values):
    scores = jnp.dot(keys_t, queries, preferred_element_type=F32)
    peak = jnp.max(scores, axis=0, keepdims=True)
    probs = jnp.exp2((scores - peak) * LOG2_SCALE).astype(BF16)
    return peak, jnp.dot(values, probs, preferred_element_type=F32)


def local_operands(i, slide_ref, q_ref, k_ref, v_ref):
    rows = q_ref.shape[1]
    slides = slide_ref.shape[0]
    tile = lanes(rows)
    head_place = lax.axis_index("head")
    query_slides = slide_ref[...]
    key_slides = (1.0 - query_slides) * F32(BLOCKED)
    extra = -(-(slides + 9) // 16) * 16 - slides
    mine = slice(i * HD, (i + 1) * HD)
    second = (tile & 3) == i
    third = (tile & 15) == 4 * head_place + i
    fourth = (tile & 63) == 4 * head_place + i
    query_extra = stack_rows(flag_rows(second) + flag_rows(third) + flag_rows(fourth), extra)
    key_extra = stack_rows(
        bias_rows(second, 2.0) + bias_rows(third, 1.5) + bias_rows(fourth, 4.0 / 3.0), extra
    )
    queries = jnp.concatenate(
        [q_ref[mine, :], jnp.concatenate([query_slides, query_extra], axis=0).astype(BF16)], axis=0
    )
    keys = jnp.concatenate(
        [k_ref[mine, :], jnp.concatenate([key_slides, key_extra], axis=0).astype(BF16)], axis=0
    )
    values = jnp.concatenate([v_ref[mine, :], jnp.ones((16, rows), BF16)], axis=0)
    return keys.T, queries, values


def local_kernel(first, slide_ref, q_ref, k_ref, v_ref, out_ref):
    for head in range(out_ref.shape[0]):
        mixed = weigh(*local_operands(first + head, slide_ref, q_ref, k_ref, v_ref))
        out_ref[head] = mixed[: HD + 8]


def count_of(kind, keys):
    return keys.shape[1] if kind == 1 else keys.shape[1] // 2 // 4 ** (kind - 2)


def with_masks(pieces, mask_at):
    placed = []
    for kind, keys, values in pieces:
        placed.append((kind, keys, values, mask_at))
        mask_at += count_of(kind, keys)
    return placed


def lay_out(pieces, k_mask_ref, k_ref, v_ref):
    features = HEADS * HD
    at = 0
    beside = []
    for kind, keys, values, mask_at in pieces:
        count = count_of(kind, keys)
        if kind == 1:
            v_ref[:features, at : at + count] = values[...]
        else:
            half = values.shape[1] // 2
            beside.append(values[:, half : half + count])
        masks = k_mask_ref[:, mask_at : mask_at + count]
        k_ref[at : at + count, :] = jnp.concatenate([keys[:, :count], masks], axis=0).T
        at += count
    if beside:
        width = sum(part.shape[1] for part in beside)
        v_ref[:features, at - width : at] = jnp.concatenate(beside, axis=1)
    v_ref[features:, :at] = jnp.ones((16, at), BF16)


def halves(ref):
    features = HEADS * HD
    return ref.at[:features, :], ref.at[features:, :]


def with_more(i, part, total, mixed):
    features = HEADS * HD
    selected = (lanes(mixed.shape[1]) & 3) == i
    return (
        part + jnp.where(selected, mixed[i * HD : (i + 1) * HD], 0.0),
        total + jnp.where(selected, mixed[features : features + 1], 0.0),
    )


def parts_of(ref, i):
    features = HEADS * HD
    return ref[i * HD : (i + 1) * HD, :], ref[features + i : features + i + 1, :]


def store_parts(ref, i, part, total):
    features = HEADS * HD
    ref[i * HD : (i + 1) * HD, :] = part
    ref[features + i : features + i + 1, :] = total


def near_pieces(kinds, one_ref, two_ref, direct):
    pieces = [(1, *halves(one_ref)), (1, *halves(two_ref))]
    return pieces + [(kind, ref, ref) for kind, ref in zip(kinds, direct)]


def last_pieces(kinds, from_beyond):
    width = from_beyond.shape[1] // len(kinds)
    passed_on = [from_beyond.at[:, at * width : (at + 1) * width] for at in range(len(kinds))]
    return [(kind, ref, ref) for kind, ref in zip(kinds, passed_on)]


def far_kernel(mask_at, q_ref, k_mask_ref, near_ref, from_one, from_two, out_ref, k_ref, v_ref):
    diagonal = [(1, *diagonal_pair(from_one, from_two))]
    lay_out(with_masks(diagonal, mask_at), k_mask_ref, k_ref, v_ref)
    mixed = weigh(k_ref[...], q_ref[...], v_ref[...])
    for i in range(HEADS):
        part, total = with_more(i, *parts_of(near_ref, i), mixed)
        store_parts(out_ref, i, part, total)


def near_kernel(kinds, q_ref, k_mask_ref, local_a, local_c, local_d, one_ref, two_ref, *refs):
    direct, (out_ref, k_ref, v_ref) = refs[:-3], refs[-3:]
    pieces = with_masks(near_pieces(kinds, one_ref, two_ref, direct), 0)
    lay_out(pieces, k_mask_ref, k_ref, v_ref)
    mixed = weigh(k_ref[...], q_ref[...], v_ref[...])
    for i in range(HEADS):
        ref = [ref.at[j] for ref in (local_a, local_c, local_d) for j in range(ref.shape[0])][i]
        store_parts(out_ref, i, *with_more(i, ref[:HD, :], ref[HD : HD + 1, :], mixed))


def add_up(head_parts, att_ref, sums_ref):
    sums = squares = None
    for i, attended in enumerate(head_parts):
        att_ref[i * HD : (i + 1) * HD, :] = attended
        head_sum = jnp.sum(attended, axis=0, keepdims=True)
        head_squares = jnp.sum(attended * attended, axis=0, keepdims=True)
        sums = head_sum if sums is None else sums + head_sum
        squares = head_squares if squares is None else squares + head_squares
    quarter = sums_ref.shape[1]
    for at in range(4):
        sums_ref[at : at + 1, :] = sums[:, at * quarter : (at + 1) * quarter]
        sums_ref[4 + at : 5 + at, :] = squares[:, at * quarter : (at + 1) * quarter]


def last_kernel(kinds, raw_refs, q_ref, k_mask_ref, near_ref, from_beyond, *refs):
    raw, (att_ref, sums_ref, k_last, v_last, k_ref, v_ref) = refs[:raw_refs], refs[raw_refs:]
    features = HEADS * HD
    own = lanes(q_ref.shape[1]) & 3
    last = last_pieces(kinds, from_beyond)
    last = with_masks(last, k_ref.shape[0] - k_last.shape[0])
    lay_out(last, k_mask_ref, k_last, v_last)
    mixed = weigh(k_last[...], q_ref[...], v_last[...])
    parts = []
    least = most = None
    for i in range(HEADS):
        part, total = with_more(i, *parts_of(near_ref, i), mixed)
        parts.append(part * (1.0 / total))
        least = total if least is None else jnp.minimum(least, total)
        most = total if most is None else jnp.maximum(most, total)
    add_up(parts, att_ref, sums_ref)
    fine = (least >= LEAST) & (most <= MOST)
    worst = jnp.max(jnp.where(fine, 0.0, 1.0))

    @pl.when(worst > 0.0)
    def _():
        slide_ref, queries, keys, values, one_ref, two_ref, from_one, from_two = raw[:8]
        pieces = near_pieces(kinds, one_ref, two_ref, raw[8:])
        pieces = with_masks(pieces + [(1, *diagonal_pair(from_one, from_two))], 0) + last
        pieces.sort(key=lambda piece: piece[0] > 1)
        lay_out(pieces, k_mask_ref, k_ref, v_ref)
        far_peak, mixed = weigh_with_peak(k_ref[...], q_ref[...], v_ref[...])
        parts = []
        for i in range(HEADS):
            mine = slice(i * HD, (i + 1) * HD)
            here, local = weigh_with_peak(*local_operands(i, slide_ref, queries, keys, values))
            there = jnp.where(own == i, far_peak, F32(BLOCKED))
            top = jnp.maximum(here, there)
            keep = jnp.exp2((here - top) * LOG2_SCALE)
            add = jnp.where(own == i, jnp.exp2((there - top) * LOG2_SCALE), F32(0.0))
            total = keep * local[HD : HD + 1] + add * mixed[features : features + 1]
            parts.append((local[:HD] * keep + mixed[mine] * add) / total)
        add_up(parts, att_ref, sums_ref)


def norm_kernel(att_ref, affine_ref, *refs):
    sum_refs, out_ref = refs[:-1], refs[-1]
    sums = sum_refs[0][...]
    for ref in sum_refs[1:]:
        sums = sums + ref[...]
    mean = sums[:4] / D
    variance = sums[4:] / D - mean * mean
    inverse = lax.rsqrt(variance + 1e-05)
    width = affine_ref.shape[2]
    quarter = mean.shape[1]
    for start in range(0, att_ref.shape[1], width):
        at, first = start // quarter, start % quarter
        part = slice(first, first + width)
        normed = (att_ref[:, start : start + width] - mean[at : at + 1, part]) * inverse[at : at + 1, part]
        out_ref[:, start : start + width] = (normed * affine_ref[0] + affine_ref[1]).astype(BF16)


def cost(flops, moved, exps=0):
    return pl.CostEstimate(flops=int(flops), bytes_accessed=int(moved), transcendentals=int(exps))


def per_device(queries, keys, values, slide_lengths, norm_gain, norm_bias):
    features, rows = queries.shape
    total_rows = rows * lax.axis_size("seq")
    spans = [min(SEG * 4**b, total_rows) // rows for b in range(4)]
    assert spans[1] == 4 and features == HEADS * HD
    pair, own = pl.pallas_call(
        pack_kernel,
        out_shape=(
            jax.ShapeDtypeStruct((2 * features, rows // 4), BF16),
            jax.ShapeDtypeStruct((features, rows // 8), BF16),
        ),
        in_specs=[HBM] * 2,
        out_specs=(VMEM,) * 2,
        scratch_shapes=[
            pltpu.VMEM((features, rows), BF16),
            pltpu.VMEM((features, rows), BF16),
            pltpu.SemaphoreType.DMA((2, HEADS)),
        ],
        compiler_params=pltpu.CompilerParams(vmem_limit_bytes=PACK_LIMIT),
        cost_estimate=cost(2 * 384 * 256 * 1024, 10**6),
        name="pack",
    )(keys, values)

    one, two = partner(pair, "seq", 1), partner(pair, "seq", 2)
    held = [(own, 0)]
    held += [(partner(own, "seq", m), m) for m in range(spans[2], spans[3], spans[2])]
    beyond = held[1:] + [
        (partner(piece, "seq", m ^ side), m ^ side ^ d)
        for m in range(0, spans[2], spans[1])
        for side in (0, 1)
        for piece, d in (held if m else held[1:] * side)
    ]
    beyond_kinds = [2 if d < spans[2] else 3 for _, d in beyond]
    kinds = [1, 1] + beyond_kinds + [1] + beyond_kinds
    distances = [1, 2] + [d for _, d in beyond] + [3] + [2 ^ d for _, d in beyond]
    counts = [rows // 4**kind for kind in kinds]
    key_count = sum(counts)
    near_count = (key_count + counts[0]) // 2
    last_count = key_count - near_count

    mask_rows = -(-(HEADS * slide_lengths.shape[0] + 8) // 16) * 16
    depth = features + mask_rows
    own_queries, key_masks, affine, slides = pl.pallas_call(
        functools.partial(mask_kernel, kinds, distances),
        out_shape=(
            jax.ShapeDtypeStruct((depth, rows), BF16),
            jax.ShapeDtypeStruct((mask_rows, key_count), BF16),
            jax.ShapeDtypeStruct((2, features, 128), F32),
            jax.ShapeDtypeStruct((slide_lengths.shape[0], rows), F32),
        ),
        in_specs=[SMEM, VMEM, VMEM, VMEM],
        out_specs=(VMEM,) * 4,
        compiler_params=PARAMS,
        cost_estimate=cost(10**8, 10**6),
        name="masks",
    )(slide_lengths, norm_gain[None, :], norm_bias[None, :], queries)

    def local(first, count, work, *operands):
        return pl.pallas_call(
            functools.partial(local_kernel, first),
            out_shape=jax.ShapeDtypeStruct((count, HD + 8, rows), F32),
            in_specs=[VMEM] * 4,
            out_specs=VMEM,
            compiler_params=PARAMS,
            cost_estimate=cost(work, 10**3),
            name="local",
        )(*operands)

    local_a = local(0, 1, 10**8, slides, queries, keys, values)
    beyond_pieces = [piece for piece, _ in beyond]
    local_a, two = lax.optimization_barrier((local_a, two))
    to_one, to_two = pl.pallas_call(
        relay_kernel,
        out_shape=(
            jax.ShapeDtypeStruct((features, rows // 4), BF16),
            jax.ShapeDtypeStruct((features, rows // 4), BF16),
        ),
        in_specs=[VMEM],
        out_specs=(VMEM,) * 2,
        compiler_params=PARAMS,
        cost_estimate=cost(0, 10**6),
        name="relay",
    )(two)
    from_one, from_two = partner(to_one, "seq", 1), partner(to_two, "seq", 1)
    held, _ = lax.optimization_barrier((queries, (to_one, to_two)))
    local_c = local(1, 1, 10**6, slides, held, keys, values)
    beyond_pieces, local_c = lax.optimization_barrier((beyond_pieces, local_c))
    to_beyond = pl.pallas_call(
        pass_kernel,
        out_shape=jax.ShapeDtypeStruct((features, rows // 8 * len(beyond)), BF16),
        in_specs=[VMEM] * len(beyond),
        out_specs=VMEM,
        compiler_params=PARAMS,
        cost_estimate=cost(0, 10**5),
        name="pass_on",
    )(*beyond_pieces)
    from_beyond = partner(to_beyond, "seq", 2)
    held, _ = lax.optimization_barrier((queries, to_beyond))
    local_d = local(2, 2, 10**6, slides, held, keys, values)

    def scratch(count):
        return [pltpu.VMEM((count, depth), BF16), pltpu.VMEM((features + 16, count), BF16)]

    near_part = pl.pallas_call(
        functools.partial(near_kernel, beyond_kinds),
        out_shape=jax.ShapeDtypeStruct((features + 8, rows), F32),
        in_specs=[VMEM] * (7 + len(beyond)),
        out_specs=VMEM,
        scratch_shapes=scratch(near_count),
        compiler_params=PARAMS,
        cost_estimate=cost(10**6, 10**4),
        name="near",
    )(own_queries, key_masks, local_a, local_c, local_d, one, two, *beyond_pieces)

    far_part = pl.pallas_call(
        functools.partial(far_kernel, near_count),
        out_shape=jax.ShapeDtypeStruct((features + 8, rows), F32),
        in_specs=[VMEM] * 5,
        out_specs=VMEM,
        scratch_shapes=scratch(counts[0]),
        compiler_params=PARAMS,
        cost_estimate=cost(10**6, 10**4),
        name="far",
    )(own_queries, key_masks, near_part, from_one, from_two)

    raw = (slides, queries, keys, values, one, two, from_one, from_two, *beyond_pieces)
    attended, sums = pl.pallas_call(
        functools.partial(last_kernel, beyond_kinds, len(raw)),
        out_shape=(
            jax.ShapeDtypeStruct((features, rows), F32),
            jax.ShapeDtypeStruct((8, rows // 4), F32),
        ),
        in_specs=[VMEM] * (4 + len(raw)),
        out_specs=(VMEM, VMEM),
        scratch_shapes=scratch(last_count - counts[0]) + scratch(key_count),
        compiler_params=PARAMS,
        cost_estimate=cost(2 * rows * last_count * 512, 10**5),
        name="last",
    )(own_queries, key_masks, far_part, from_beyond, *raw)

    all_sums = [sums] + [partner(sums, "head", m) for m in range(1, lax.axis_size("head"))]
    return pl.pallas_call(
        norm_kernel,
        out_shape=jax.ShapeDtypeStruct((features, rows), BF16),
        in_specs=[VMEM] * (2 + len(all_sums)),
        out_specs=VMEM,
        compiler_params=PARAMS,
        name="norm",
    )(attended, affine, *all_sums)


def solution(mesh):
    placed = (P("head", "seq"), P("head", "seq"), P("head", "seq"), P(), P("head"), P("head"))
    return jax.shard_map(
        per_device, mesh=mesh, in_specs=placed, out_specs=P("head", "seq"), check_vma=False
    )
```

```python
import functools
import math

import jax
import jax.numpy as jnp
import numpy as np
from jax import lax
from jax.experimental import pallas as pl
from jax.experimental.pallas import tpu as pltpu
from jax.sharding import PartitionSpec as P

D = 768
HD = 48
SEG = 1024
HEADS = 4
BLOCKED = -1e30
SCALE = 1.0 / math.sqrt(HD)
LOG2_SCALE = math.log2(math.e) * SCALE
LEAST, MOST = 1e-20, 1e30
F32 = jnp.float32
BF16 = jnp.bfloat16
HBM = pl.BlockSpec(memory_space=pltpu.HBM)
VMEM = pl.BlockSpec(memory_space=pltpu.VMEM)
SMEM = pl.BlockSpec(memory_space=pltpu.SMEM)
PACK_LIMIT = 107 * 2**19
PARAMS = pltpu.CompilerParams(vmem_limit_bytes=40 * 2**20)


def partner(value, axis, mask):
    pairs = [(source, source ^ mask) for source in range(lax.axis_size(axis))]
    return lax.ppermute(value, axis, pairs)


def thirds(value):
    parts = []
    for _ in range(3):
        part = float(np.asarray(value, jnp.bfloat16))
        parts.append(part)
        value -= part
    return parts


def bias_rows(flags, factor):
    return [jnp.where(flags, F32(part), F32(0.0)) for part in thirds(math.log(factor) / SCALE)]


def flag_rows(flags):
    return [jnp.where(flags, F32(1.0), F32(0.0))] * 3


def slide_of(positions, lengths_ref):
    slide = jnp.zeros(positions.shape, jnp.int32)
    end = jnp.int32(0)
    for k in range(lengths_ref.shape[0]):
        end = end + lengths_ref[k]
        slide = slide + jnp.where(positions >= end, 1, 0)
    return slide


def stack_rows(rows, count):
    width = rows[0].shape[1]
    index = lax.broadcasted_iota(jnp.int32, (count, width), 0)
    block = jnp.zeros((count, width), F32)
    for k, row in enumerate(rows):
        block = jnp.where(index == k, row, block)
    return block


def lanes(width):
    return lax.broadcasted_iota(jnp.int32, (1, width), 1)


def compact_index(place, head_place):
    quarter = place >> 6
    return 16 * (place & 15) + 4 * ((place >> 4) & 3) + ((quarter + head_place) & 3)


def only_head(ref, own):
    width = ref.shape[1]
    return [
        ref[i * HD : (i + 1) * HD, :]
        * jnp.broadcast_to(jnp.where(own == i, F32(1.0), F32(0.0)), (HD, width)).astype(BF16)
        for i in range(HEADS)
    ]


def pack_kernel(k_hbm, v_hbm, pair_ref, sixteenth_ref, *scratch):
    targets, arrived = scratch[:2], scratch[2]
    copies = []
    for at, (source, target) in enumerate(zip((k_hbm, v_hbm), targets)):
        for i in range(HEADS):
            part = pl.ds(i * HD, HD)
            copies.append(
                pltpu.make_async_copy(source.at[part, :], target.at[part, :], arrived.at[at, i])
            )
    for copy in copies:
        copy.start()
    features, rows = targets[0].shape
    packed = rows // 4
    head_place = lax.axis_index("head")
    group = lax.broadcasted_iota(jnp.int32, (rows, packed), 0) >> 2
    place = lax.broadcasted_iota(jnp.int32, (rows, packed), 1)
    pick = jnp.where(compact_index(place, head_place) == group, F32(1.0), F32(0.0)).astype(BF16)
    own = lanes(rows) & 3
    results = []
    for at, ref in enumerate(targets):
        for copy in copies[at * HEADS : (at + 1) * HEADS]:
            copy.wait()
        masked = jnp.concatenate(only_head(ref, own), axis=0)
        compact = jnp.dot(masked, pick, preferred_element_type=F32)
        pair_ref[at * features : (at + 1) * features, :] = compact.astype(BF16)
        results.append(compact[:, : packed // 4])
    sixteenth_ref[...] = jnp.concatenate(results, axis=1).astype(BF16)


def relay_kernel(two_ref, to_one, to_two):
    half = to_two.shape[0]
    to_one[...] = two_ref[half:, :]
    to_two[...] = two_ref[:half, :]


def pass_kernel(*refs):
    out = refs[-1]
    at = 0
    for piece in refs[:-1]:
        out[:, at : at + piece.shape[1]] = piece[...]
        at += piece.shape[1]


def diagonal_pair(from_one, from_two):
    return from_two, from_one


def mask_kernel(kinds, distances, lengths_ref, gain_ref, bias_ref, q_ref, q_out, k_mask_out, affine_out, slide_out):
    rows = q_ref.shape[1]
    features = HEADS * HD
    slides = lengths_ref.shape[0]
    tile = lanes(rows)
    seq_place = lax.axis_index("seq")
    head_place = lax.axis_index("head")
    extra = k_mask_out.shape[0] - HEADS * slides

    counts = [rows // 4**kind for kind in kinds]
    total = sum(counts)
    first = jnp.concatenate(
        [
            (seq_place ^ distance) * rows + 4 * compact_index(lanes(count), head_place)
            for count, distance in zip(counts, distances)
        ],
        axis=1,
    )
    slide = slide_of(first + lax.broadcasted_iota(jnp.int32, (HEADS, total), 0), lengths_ref)
    row = lax.broadcasted_iota(jnp.int32, (slides, total), 0)
    masks = [jnp.where(slide[i : i + 1] == row, F32(0.0), F32(BLOCKED)) for i in range(HEADS)]
    added = []
    for kind, count in zip(kinds, counts):
        place = lanes(count)
        none = jnp.zeros((1, count), F32)
        in_third = place < rows // 16
        in_fourth = place < rows // 64
        if kind == 1:
            extras = bias_rows(in_third, 2.0) + bias_rows(in_fourth, 1.5) + [none, none]
        elif kind == 2:
            extras = [none] * 3 + bias_rows(in_fourth, 2.0) + [none + BLOCKED, none]
        else:
            extras = [none] * 6 + [none, none + BLOCKED]
        added.append(stack_rows(extras, extra))
    masks.append(jnp.concatenate(added, axis=1))
    k_mask_out[...] = jnp.concatenate(masks, axis=0).astype(BF16)

    slide = slide_of(seq_place * rows + tile, lengths_ref)
    same = slide == lax.broadcasted_iota(jnp.int32, (slides, rows), 0)
    slide_out[...] = jnp.where(same, F32(1.0), F32(0.0))
    masks = [jnp.where(same & ((tile & 3) == i), F32(1.0), F32(0.0)) for i in range(HEADS)]
    third = ((tile >> 2) & 3) == head_place
    fourth = ((tile >> 2) & 15) == head_place
    masks.append(
        stack_rows(
            flag_rows(third) + flag_rows(fourth) + flag_rows(~third)[:1] + flag_rows(~fourth)[:1],
            extra,
        )
    )
    q_out[:features, :] = jnp.concatenate(only_head(q_ref, tile & 3), axis=0)
    q_out[features:, :] = jnp.concatenate(masks, axis=0).astype(BF16)

    r = lax.broadcasted_iota(jnp.int32, (features, features), 0)
    c = lax.broadcasted_iota(jnp.int32, (features, features), 1)
    for at, ref in enumerate((gain_ref, bias_ref)):
        column = jnp.sum(jnp.where(r == c, ref[...], 0.0), axis=1, keepdims=True)
        affine_out[at] = jnp.broadcast_to(column, (features, 128))


def weigh(keys_t, queries, values):
    scores = jnp.dot(keys_t, queries, preferred_element_type=F32)
    probs = jnp.exp2(scores * LOG2_SCALE).astype(BF16)
    return jnp.dot(values, probs, preferred_element_type=F32)


def weigh_with_peak(keys_t, queries, values):
    scores = jnp.dot(keys_t, queries, preferred_element_type=F32)
    peak = jnp.max(scores, axis=0, keepdims=True)
    probs = jnp.exp2((scores - peak) * LOG2_SCALE).astype(BF16)
    return peak, jnp.dot(values, probs, preferred_element_type=F32)


def local_operands(i, slide_ref, q_ref, k_ref, v_ref):
    rows = q_ref.shape[1]
    slides = slide_ref.shape[0]
    tile = lanes(rows)
    head_place = lax.axis_index("head")
    query_slides = slide_ref[...]
    key_slides = (1.0 - query_slides) * F32(BLOCKED)
    extra = -(-(slides + 9) // 16) * 16 - slides
    mine = slice(i * HD, (i + 1) * HD)
    second = (tile & 3) == i
    third = (tile & 15) == 4 * head_place + i
    fourth = (tile & 63) == 4 * head_place + i
    query_extra = stack_rows(flag_rows(second) + flag_rows(third) + flag_rows(fourth), extra)
    key_extra = stack_rows(
        bias_rows(second, 2.0) + bias_rows(third, 1.5) + bias_rows(fourth, 4.0 / 3.0), extra
    )
    queries = jnp.concatenate(
        [q_ref[mine, :], jnp.concatenate([query_slides, query_extra], axis=0).astype(BF16)], axis=0
    )
    keys = jnp.concatenate(
        [k_ref[mine, :], jnp.concatenate([key_slides, key_extra], axis=0).astype(BF16)], axis=0
    )
    values = jnp.concatenate([v_ref[mine, :], jnp.ones((16, rows), BF16)], axis=0)
    return keys.T, queries, values


def local_kernel(first, slide_ref, q_ref, k_ref, v_ref, out_ref):
    for head in range(out_ref.shape[0]):
        mixed = weigh(*local_operands(first + head, slide_ref, q_ref, k_ref, v_ref))
        out_ref[head] = mixed[: HD + 8]


def count_of(kind, keys):
    return keys.shape[1] if kind == 1 else keys.shape[1] // 2 // 4 ** (kind - 2)


def with_masks(pieces, mask_at):
    placed = []
    for kind, keys, values in pieces:
        placed.append((kind, keys, values, mask_at))
        mask_at += count_of(kind, keys)
    return placed


def lay_out(pieces, k_mask_ref, k_ref, v_ref):
    features = HEADS * HD
    at = 0
    beside = []
    for kind, keys, values, mask_at in pieces:
        count = count_of(kind, keys)
        if kind == 1:
            v_ref[:features, at : at + count] = values[...]
        else:
            half = values.shape[1] // 2
            beside.append(values[:, half : half + count])
        masks = k_mask_ref[:, mask_at : mask_at + count]
        k_ref[at : at + count, :] = jnp.concatenate([keys[:, :count], masks], axis=0).T
        at += count
    if beside:
        width = sum(part.shape[1] for part in beside)
        v_ref[:features, at - width : at] = jnp.concatenate(beside, axis=1)
    v_ref[features:, :at] = jnp.ones((16, at), BF16)


def halves(ref):
    features = HEADS * HD
    return ref.at[:features, :], ref.at[features:, :]


def with_more(i, part, total, mixed):
    features = HEADS * HD
    selected = (lanes(mixed.shape[1]) & 3) == i
    return (
        part + jnp.where(selected, mixed[i * HD : (i + 1) * HD], 0.0),
        total + jnp.where(selected, mixed[features : features + 1], 0.0),
    )


def parts_of(ref, i):
    features = HEADS * HD
    return ref[i * HD : (i + 1) * HD, :], ref[features + i : features + i + 1, :]


def store_parts(ref, i, part, total):
    features = HEADS * HD
    ref[i * HD : (i + 1) * HD, :] = part
    ref[features + i : features + i + 1, :] = total


def near_pieces(kinds, one_ref, two_ref, direct):
    pieces = [(1, *halves(one_ref)), (1, *halves(two_ref))]
    return pieces + [(kind, ref, ref) for kind, ref in zip(kinds, direct)]


def last_pieces(kinds, from_beyond):
    width = from_beyond.shape[1] // len(kinds)
    passed_on = [from_beyond.at[:, at * width : (at + 1) * width] for at in range(len(kinds))]
    return [(kind, ref, ref) for kind, ref in zip(kinds, passed_on)]


def far_kernel(mask_at, q_ref, k_mask_ref, near_ref, from_one, from_two, out_ref, k_ref, v_ref):
    diagonal = [(1, *diagonal_pair(from_one, from_two))]
    lay_out(with_masks(diagonal, mask_at), k_mask_ref, k_ref, v_ref)
    mixed = weigh(k_ref[...], q_ref[...], v_ref[...])
    for i in range(HEADS):
        part, total = with_more(i, *parts_of(near_ref, i), mixed)
        store_parts(out_ref, i, part, total)


def near_kernel(kinds, q_ref, k_mask_ref, local_a, local_c, local_d, one_ref, two_ref, *refs):
    direct, (out_ref, k_ref, v_ref) = refs[:-3], refs[-3:]
    pieces = with_masks(near_pieces(kinds, one_ref, two_ref, direct), 0)
    lay_out(pieces, k_mask_ref, k_ref, v_ref)
    mixed = weigh(k_ref[...], q_ref[...], v_ref[...])
    for i in range(HEADS):
        ref = [ref.at[j] for ref in (local_a, local_c, local_d) for j in range(ref.shape[0])][i]
        store_parts(out_ref, i, *with_more(i, ref[:HD, :], ref[HD : HD + 1, :], mixed))


def add_up(head_parts, att_ref, sums_ref):
    sums = squares = None
    for i, attended in enumerate(head_parts):
        att_ref[i * HD : (i + 1) * HD, :] = attended
        head_sum = jnp.sum(attended, axis=0, keepdims=True)
        head_squares = jnp.sum(attended * attended, axis=0, keepdims=True)
        sums = head_sum if sums is None else sums + head_sum
        squares = head_squares if squares is None else squares + head_squares
    quarter = sums_ref.shape[1]
    for at in range(4):
        sums_ref[at : at + 1, :] = sums[:, at * quarter : (at + 1) * quarter]
        sums_ref[4 + at : 5 + at, :] = squares[:, at * quarter : (at + 1) * quarter]


def last_kernel(kinds, raw_refs, q_ref, k_mask_ref, near_ref, from_beyond, *refs):
    raw, (att_ref, sums_ref, k_last, v_last, k_ref, v_ref) = refs[:raw_refs], refs[raw_refs:]
    features = HEADS * HD
    own = lanes(q_ref.shape[1]) & 3
    last = last_pieces(kinds, from_beyond)
    last = with_masks(last, k_ref.shape[0] - k_last.shape[0])
    lay_out(last, k_mask_ref, k_last, v_last)
    mixed = weigh(k_last[...], q_ref[...], v_last[...])
    sets = [with_more(i, *parts_of(near_ref, i), mixed) for i in range(HEADS)]
    totals = [total for _, total in sets]
    least, most = functools.reduce(jnp.minimum, totals), functools.reduce(jnp.maximum, totals)
    worst = jnp.max(jnp.where((least >= LEAST) & (most <= MOST), 0.0, 1.0))
    add_up([part * (1.0 / total) for part, total in sets], att_ref, sums_ref)

    @pl.when(worst > 0.0)
    def _():
        slide_ref, queries, keys, values, one_ref, two_ref, from_one, from_two = raw[:8]
        pieces = near_pieces(kinds, one_ref, two_ref, raw[8:])
        pieces = with_masks(pieces + [(1, *diagonal_pair(from_one, from_two))], 0) + last
        pieces.sort(key=lambda piece: piece[0] > 1)
        lay_out(pieces, k_mask_ref, k_ref, v_ref)
        far_peak, mixed = weigh_with_peak(k_ref[...], q_ref[...], v_ref[...])
        parts = []
        for i in range(HEADS):
            mine = slice(i * HD, (i + 1) * HD)
            here, local = weigh_with_peak(*local_operands(i, slide_ref, queries, keys, values))
            there = jnp.where(own == i, far_peak, F32(BLOCKED))
            top = jnp.maximum(here, there)
            keep = jnp.exp2((here - top) * LOG2_SCALE)
            add = jnp.where(own == i, jnp.exp2((there - top) * LOG2_SCALE), F32(0.0))
            total = keep * local[HD : HD + 1] + add * mixed[features : features + 1]
            parts.append((local[:HD] * keep + mixed[mine] * add) / total)
        add_up(parts, att_ref, sums_ref)


def norm_kernel(att_ref, affine_ref, *refs):
    sum_refs, out_ref = refs[:-1], refs[-1]
    sums = sum_refs[0][...]
    for ref in sum_refs[1:]:
        sums = sums + ref[...]
    mean = sums[:4] / D
    variance = sums[4:] / D - mean * mean
    inverse = lax.rsqrt(variance + 1e-05)
    width = affine_ref.shape[2]
    quarter = mean.shape[1]
    for start in range(0, att_ref.shape[1], width):
        at, first = start // quarter, start % quarter
        part = slice(first, first + width)
        normed = (att_ref[:, start : start + width] - mean[at : at + 1, part]) * inverse[at : at + 1, part]
        out_ref[:, start : start + width] = (normed * affine_ref[0] + affine_ref[1]).astype(BF16)


def cost(flops, moved, exps=0):
    return pl.CostEstimate(flops=int(flops), bytes_accessed=int(moved), transcendentals=int(exps))


def per_device(queries, keys, values, slide_lengths, norm_gain, norm_bias):
    features, rows = queries.shape
    total_rows = rows * lax.axis_size("seq")
    spans = [min(SEG * 4**b, total_rows) // rows for b in range(4)]
    assert spans[1] == 4 and features == HEADS * HD
    pair, own = pl.pallas_call(
        pack_kernel,
        out_shape=(
            jax.ShapeDtypeStruct((2 * features, rows // 4), BF16),
            jax.ShapeDtypeStruct((features, rows // 8), BF16),
        ),
        in_specs=[HBM] * 2,
        out_specs=(VMEM,) * 2,
        scratch_shapes=[
            pltpu.VMEM((features, rows), BF16),
            pltpu.VMEM((features, rows), BF16),
            pltpu.SemaphoreType.DMA((2, HEADS)),
        ],
        compiler_params=pltpu.CompilerParams(vmem_limit_bytes=PACK_LIMIT),
        cost_estimate=cost(2 * 384 * 256 * 1024, 10**6),
        name="pack",
    )(keys, values)

    one, two = partner(pair, "seq", 1), partner(pair, "seq", 2)
    held = [(own, 0)]
    held += [(partner(own, "seq", m), m) for m in range(spans[2], spans[3], spans[2])]
    beyond = held[1:] + [
        (partner(piece, "seq", m ^ side), m ^ side ^ d)
        for m in range(0, spans[2], spans[1])
        for side in (0, 1)
        for piece, d in (held if m else held[1:] * side)
    ]
    beyond_kinds = [2 if d < spans[2] else 3 for _, d in beyond]
    kinds = [1, 1] + beyond_kinds + [1] + beyond_kinds
    distances = [1, 2] + [d for _, d in beyond] + [3] + [2 ^ d for _, d in beyond]
    counts = [rows // 4**kind for kind in kinds]
    key_count = sum(counts)
    near_count = (key_count + counts[0]) // 2
    last_count = key_count - near_count

    mask_rows = -(-(HEADS * slide_lengths.shape[0] + 8) // 16) * 16
    depth = features + mask_rows
    own_queries, key_masks, affine, slides = pl.pallas_call(
        functools.partial(mask_kernel, kinds, distances),
        out_shape=(
            jax.ShapeDtypeStruct((depth, rows), BF16),
            jax.ShapeDtypeStruct((mask_rows, key_count), BF16),
            jax.ShapeDtypeStruct((2, features, 128), F32),
            jax.ShapeDtypeStruct((slide_lengths.shape[0], rows), F32),
        ),
        in_specs=[SMEM, VMEM, VMEM, VMEM],
        out_specs=(VMEM,) * 4,
        compiler_params=PARAMS,
        cost_estimate=cost(10**8, 10**6),
        name="masks",
    )(slide_lengths, norm_gain[None, :], norm_bias[None, :], queries)

    def local(first, count, work, *operands):
        return pl.pallas_call(
            functools.partial(local_kernel, first),
            out_shape=jax.ShapeDtypeStruct((count, HD + 8, rows), F32),
            in_specs=[VMEM] * 4,
            out_specs=VMEM,
            compiler_params=PARAMS,
            cost_estimate=cost(work, 10**3),
            name="local",
        )(*operands)

    local_a = local(0, 1, 10**8, slides, queries, keys, values)
    beyond_pieces = [piece for piece, _ in beyond]
    local_a, two = lax.optimization_barrier((local_a, two))
    to_one, to_two = pl.pallas_call(
        relay_kernel,
        out_shape=(
            jax.ShapeDtypeStruct((features, rows // 4), BF16),
            jax.ShapeDtypeStruct((features, rows // 4), BF16),
        ),
        in_specs=[VMEM],
        out_specs=(VMEM,) * 2,
        compiler_params=PARAMS,
        cost_estimate=cost(0, 10**6),
        name="relay",
    )(two)
    from_one, from_two = partner(to_one, "seq", 1), partner(to_two, "seq", 1)
    held, _ = lax.optimization_barrier((queries, (to_one, to_two)))
    local_c = local(1, 1, 10**6, slides, held, keys, values)
    beyond_pieces, local_c = lax.optimization_barrier((beyond_pieces, local_c))
    to_beyond = pl.pallas_call(
        pass_kernel,
        out_shape=jax.ShapeDtypeStruct((features, rows // 8 * len(beyond)), BF16),
        in_specs=[VMEM] * len(beyond),
        out_specs=VMEM,
        compiler_params=PARAMS,
        cost_estimate=cost(0, 10**5),
        name="pass_on",
    )(*beyond_pieces)
    from_beyond = partner(to_beyond, "seq", 2)
    held, _ = lax.optimization_barrier((queries, to_beyond))
    local_d = local(2, 2, 10**6, slides, held, keys, values)

    def scratch(count):
        return [pltpu.VMEM((count, depth), BF16), pltpu.VMEM((features + 16, count), BF16)]

    near_part = pl.pallas_call(
        functools.partial(near_kernel, beyond_kinds),
        out_shape=jax.ShapeDtypeStruct((features + 8, rows), F32),
        in_specs=[VMEM] * (7 + len(beyond)),
        out_specs=VMEM,
        scratch_shapes=scratch(near_count),
        compiler_params=PARAMS,
        cost_estimate=cost(10**6, 10**4),
        name="near",
    )(own_queries, key_masks, local_a, local_c, local_d, one, two, *beyond_pieces)

    far_part = pl.pallas_call(
        functools.partial(far_kernel, near_count),
        out_shape=jax.ShapeDtypeStruct((features + 8, rows), F32),
        in_specs=[VMEM] * 5,
        out_specs=VMEM,
        scratch_shapes=scratch(counts[0]),
        compiler_params=PARAMS,
        cost_estimate=cost(10**6, 10**4),
        name="far",
    )(own_queries, key_masks, near_part, from_one, from_two)

    raw = (slides, queries, keys, values, one, two, from_one, from_two, *beyond_pieces)
    attended, sums = pl.pallas_call(
        functools.partial(last_kernel, beyond_kinds, len(raw)),
        out_shape=(
            jax.ShapeDtypeStruct((features, rows), F32),
            jax.ShapeDtypeStruct((8, rows // 4), F32),
        ),
        in_specs=[VMEM] * (4 + len(raw)),
        out_specs=(VMEM, VMEM),
        scratch_shapes=scratch(last_count - counts[0]) + scratch(key_count),
        compiler_params=PARAMS,
        cost_estimate=cost(2 * rows * last_count * 512, 10**5),
        name="last",
    )(own_queries, key_masks, far_part, from_beyond, *raw)

    all_sums = [sums] + [partner(sums, "head", m) for m in range(1, lax.axis_size("head"))]
    return pl.pallas_call(
        norm_kernel,
        out_shape=jax.ShapeDtypeStruct((features, rows), BF16),
        in_specs=[VMEM] * (2 + len(all_sums)),
        out_specs=VMEM,
        compiler_params=PARAMS,
        name="norm",
    )(attended, affine, *all_sums)


def solution(mesh):
    placed = (P("head", "seq"), P("head", "seq"), P("head", "seq"), P(), P("head"), P("head"))
    return jax.shard_map(
        per_device, mesh=mesh, in_specs=placed, out_specs=P("head", "seq"), check_vma=False
    )
```
